256 devices in a mesh: dp: 8 (over x, core), expert: 32 (over z, y).
Axes of the slice: x: 4, y: 4, z: 8, core: 2. Of those that a mesh axis runs over, the one named last changes fastest.
Arguments:
- features: bfloat16 [65536, 2048], P(('dp', 'expert')), may hold values from -6 to 6
- expert_ids: int32 [65536, 2], P(('dp', 'expert')), may hold values from 0 to 31, all different within a row; in each aligned block of 256 rows (0 to 255, 256 to 511, ...) at most 32 rows name the same one
- gate_weights: float32 [65536, 2], P(('dp', 'expert')), may hold values from 0.1 to 1
- out_grads: bfloat16 [65536, 2, 1536], P(('dp', 'expert')), may hold values from -6 to 6
Outputs:
- input_factor: float32 [32, 2048, 2048], P('expert', 'dp')
- grad_factor: float32 [32, 1536, 1536], P('expert', 'dp')
The draws below stay inside these ranges and needn't reach their ends.
Inputs may be any that keep to these rules, and one draw needn't show every extreme that they name: `expert_ids`: each row names 2 different experts. Among the 256 tokens of one device no expert is named by more than 32 rows, a bound that some block reaches.
All inputs are finite; a program needn't handle non-finite values.
Results may differ from the reference program's by a relative error of at most 0.0027.
Values may be sent and summed in bfloat16 or wider, within the bound.
A program may use at most 128 MiB of HBM per device.

```python
import math
import jax
import jax.numpy as jnp
import numpy as np
from jax import lax

DW = 2048
HID = 1536
TOP = 2
TOK_DEV = 256
EXPERTS = 32
CAP = 32
TOKENS = 65536
N_DP = 8
N_EXPERT = 32


def block_levels(key, shape, cuts, smallest, largest):
    factor_of = 1.0
    for dim, shards_of in cuts:
        heights = jax.random.uniform(jax.random.fold_in(jax.random.fold_in(key, 6), dim), (shards_of,), jnp.float32, smallest / len(cuts), largest / len(cuts))
        factor_of = factor_of * jnp.repeat(jnp.exp(heights), shape[dim] // shards_of).reshape((-1,) + (1,) * (len(shape) - 1 - dim))
    return factor_of


def deal_out(own_key, own, number, rows, amount, top, most, skew):
    ranking = jax.random.permutation(own_key, amount)
    crowded, usual = load_shares(amount, rows * top, most, skew, True), load_shares(amount, rows * top, most, skew, False)
    places = jnp.arange(amount)

    def named(sizes, turn):
        used = int((sizes > 0).sum())
        fixed = max(1, used // 4)
        passed = fixed + (places - fixed + turn * (used - fixed)) % max(1, amount - fixed)
        return jnp.zeros((amount,), jnp.int32).at[ranking[jnp.where(places < fixed, places, passed)]].set(jnp.asarray(sizes, jnp.int32))

    sizes = jnp.where(number % 4 == 0, named(crowded, number // 4), named(usual, number - number // 4 - 1))
    mixed = jax.random.permutation(jax.random.fold_in(own, 3), amount)
    giver, receiver = mixed[0:amount // 2 * 2:2], mixed[1:amount // 2 * 2:2]
    margin = jnp.minimum(sizes[giver] - 1, most - sizes[receiver]) // 2
    margin = jnp.where((giver == ranking[0]) | (receiver == ranking[0]) | (sizes[receiver] == 0), 0, jnp.maximum(margin, 0))
    passed = jax.random.randint(jax.random.fold_in(own, 4), (amount // 2,), 0, 1 << 20) % (margin + 1)
    sizes = sizes.at[giver].add(-passed).at[receiver].add(passed)
    labels = jnp.searchsorted(jnp.cumsum(sizes), jnp.arange(rows * top), side="right").astype(jnp.int32)
    grid = labels.reshape(top, rows).T
    grid = grid[jax.random.permutation(jax.random.fold_in(own, 1), rows)]
    turn = jax.random.randint(jax.random.fold_in(own, 2), (rows, 1), 0, top)
    return jnp.take_along_axis(grid, (jnp.arange(top)[None, :] + turn) % top, axis=1)


def load_shares(count, total, reach, skew, full):
    weights = [(1 << 20) // math.isqrt(rank ** skew) + 1 for rank in range(1, count + 1)]
    largest = reach if full else min(reach, max(-(-total // count), total * weights[0] // sum(weights)))
    least = 1 if total - largest >= count - 1 else 0
    given, rest = [largest] + [least] * (count - 1), total - largest - least * (count - 1)
    while rest > 0:
        candidates = [i for i in range(1, count) if given[i] < largest] or [i for i in range(1, count) if given[i] < reach]
        pool, left = sum([weights[i] for i in candidates]), rest
        for i in candidates:
            extra = min(reach - given[i], max(1, left * weights[i] // pool), rest)
            given[i] = given[i] + extra
            rest = rest - extra
    return np.array(given)


def scatter_about(rng, shape, spread, reach, shards=(), held_as=jnp.bfloat16):
    result = spread * jax.random.normal(rng, shape, jnp.float32)
    if shards:
        result = result * block_levels(rng, shape, shards, -0.22, 0.18)
    return jnp.clip(result, -reach, reach).astype(held_as)


def setup_inputs(seed: int = 0) -> dict:
    streams_of = jax.random.split(jax.random.key(seed), 5)
    features = scatter_about(streams_of[0], (TOKENS, DW), 1.0, 6.0, ((0, 256),))
    expert_ids_keys = jax.random.split(jax.random.fold_in(streams_of[1], 1), TOKENS // TOK_DEV)
    expert_ids_turns = jax.random.permutation(jax.random.fold_in(streams_of[1], 3), TOKENS // TOK_DEV)
    expert_ids = jax.vmap(lambda own, number: deal_out(jax.random.fold_in(streams_of[1], 2), own, number, TOK_DEV, EXPERTS, TOP, CAP, 2))(expert_ids_keys, expert_ids_turns).reshape((TOKENS, TOP))
    gate_weights = jnp.clip(jnp.exp(math.log(1.0) - 2.3025851 * jax.random.uniform(streams_of[2], (TOKENS, TOP), jnp.float32) ** block_levels(streams_of[2], (TOKENS, TOP), ((0, 256),), -0.2, 0.2)), 0.1, 1.0)
    out_grads = scatter_about(streams_of[3], (TOKENS, TOP, HID), 1.0, 6.0, ((0, 256),))
    return {"features": features, "expert_ids": expert_ids, "gate_weights": gate_weights, "out_grads": out_grads}


def dispatch(features, expert_ids, gate_weights, out_grads, experts, capacity):
    tokens, routes = expert_ids.shape
    pairs = tokens * routes
    flat_ids = expert_ids.reshape(pairs)
    onehot = (flat_ids[:, None] == jnp.arange(experts, dtype=jnp.int32)[None, :]).astype(jnp.int32)
    earlier = jnp.cumsum(onehot, axis=0) - onehot
    position = jnp.sum(earlier * onehot, axis=1).astype(jnp.int32)
    target = (flat_ids * capacity + position).astype(jnp.int32)
    source = jnp.full((experts * capacity,), pairs, jnp.int32).at[target].set(jnp.arange(pairs, dtype=jnp.int32))
    padded_rows = jnp.concatenate([features, jnp.zeros((1, features.shape[1]), features.dtype)], axis=0)
    scaled = (out_grads.astype(jnp.float32) * gate_weights[:, :, None]).astype(jnp.bfloat16)
    scaled = scaled.reshape(pairs, out_grads.shape[2])
    padded_grads = jnp.concatenate([scaled, jnp.zeros((1, scaled.shape[1]), scaled.dtype)], axis=0)
    sent_rows = padded_rows[source // routes].reshape(experts, capacity, features.shape[1])
    sent_grads = padded_grads[source].reshape(experts, capacity, scaled.shape[1])
    return sent_rows, sent_grads


def reference(features, expert_ids, gate_weights, out_grads):
    feats = features.reshape(N_DP, N_EXPERT, TOK_DEV, DW)
    ids = expert_ids.reshape(N_DP, N_EXPERT, TOK_DEV, TOP)
    gates = gate_weights.reshape(N_DP, N_EXPERT, TOK_DEV, TOP)
    grads = out_grads.reshape(N_DP, N_EXPERT, TOK_DEV, TOP, HID)
    scale = 1.0 / (2 * TOK_DEV * TOP)

    def route_one(feat_block, id_block, gate_block, grad_block):
        return dispatch(feat_block, id_block, gate_block, grad_block, EXPERTS, CAP)

    def one_group(totals, group):
        g_feats, g_ids, g_gates, g_grads = group
        sent_rows, sent_grads = jax.vmap(route_one)(g_feats, g_ids, g_gates, g_grads)
        rows_by_expert = jnp.swapaxes(sent_rows, 0, 1).reshape(EXPERTS, N_EXPERT * CAP, DW)
        grads_by_expert = jnp.swapaxes(sent_grads, 0, 1).reshape(EXPERTS, N_EXPERT * CAP, HID)

        def gram(pair):
            rows_here, grads_here = pair
            first = scale * jnp.dot(rows_here.T, rows_here, preferred_element_type=jnp.float32)
            second = scale * jnp.dot(grads_here.T, grads_here, preferred_element_type=jnp.float32)
            return first, second

        inputs_part, grads_part = lax.map(gram, (rows_by_expert, grads_by_expert))
        return (totals[0] + inputs_part, totals[1] + grads_part), None

    init = (jnp.zeros((EXPERTS, DW, DW), jnp.float32), jnp.zeros((EXPERTS, HID, HID), jnp.float32))
    (input_factor, grad_factor), _ = lax.scan(one_group, init, (feats, ids, gates, grads))
    return input_factor, grad_factor
```

```python
import jax
import jax.numpy as jnp
from jax import lax
from jax.experimental import pallas as pl
from jax.experimental.pallas import tpu as pltpu
from jax.sharding import PartitionSpec as P

MESH = pl.DeviceIdType.MESH
BF = jnp.bfloat16
F32 = jnp.float32

N_DP = 8
N_Z = 8
N_Y = 4
E = 32
CAP = 32
ROWS = E * CAP
W = 512
SUB = 64
SCALE = 1.0 / 1024.0


def make_panels(nf, ng):
    panels = []
    ub = tb = 0
    for kind, count in (("f", nf), ("g", ng)):
        for j in range(count):
            panels.append(dict(kind=kind, J=j, ub=ub, tb=tb, first=len(panels) - j))
            ub += j + 1
            tb += j
    return panels, ub, tb


PANELS, UNITS, TUNITS = make_panels(4, 3)
NP = len(PANELS)
AHEAD = 2


def kernel(
    feat, grad, ids, of, og,
    sel, self_f, sb, rb, gram, rsd, rsu, st, ts, tr, tt,
    a_send, a_recv, d_send, d_recv, u_send, u_recv, t_send, t_recv, m_send, m_recv,
):
    dp = lax.axis_index("dp")
    ex = lax.axis_index("expert")
    z = ex // N_Y
    y = ex % N_Y
    me = dp * N_Y + y

    def plane_peer(r):
        q = (me + r) % E
        return q, (q // N_Y, z * N_Y + q % N_Y)

    down = (dp, ((z + N_Z - 1) % N_Z) * N_Y + y)
    up = (dp, ((z + 1) % N_Z) * N_Y + y)
    mirror = (z, dp * N_Y + y)

    barrier = pltpu.get_barrier_semaphore()

    def greet(r, c):
        pl.semaphore_signal(barrier, inc=1, device_id=plane_peer(r)[1], device_id_type=MESH)
        return c

    lax.fori_loop(1, E, greet, 0)
    pl.semaphore_signal(barrier, inc=1, device_id=down, device_id_type=MESH)
    pl.semaphore_signal(barrier, inc=1, device_id=up, device_id_type=MESH)

    @pl.when(dp != z)
    def _():
        pl.semaphore_signal(barrier, inc=1, device_id=mirror, device_id_type=MESH)

    pairs = ids.shape[1]
    idv = ids[...]
    hot = lax.broadcasted_iota(jnp.int32, (E, pairs), 0) == idv
    hot = jnp.where(hot, 1.0, 0.0)
    tri = lax.broadcasted_iota(jnp.int32, (pairs, pairs), 0) < lax.broadcasted_iota(
        jnp.int32, (pairs, pairs), 1
    )
    tri = jnp.where(tri, 1.0, 0.0).astype(BF)
    earlier = jnp.dot(hot.astype(BF), tri, preferred_element_type=F32)
    pos = jnp.sum(earlier * hot, axis=0, keepdims=True)
    target = idv * CAP + pos.astype(jnp.int32)
    chunk = 128

    def build_sel(i, c):
        r0 = pl.multiple_of(i * chunk, chunk)
        m = lax.broadcasted_iota(jnp.int32, (chunk, pairs), 0) + r0 == target
        m = jnp.where(m, 1.0, 0.0)
        sel[pl.ds(r0, chunk), :] = m.astype(BF)
        self_f[pl.ds(r0, chunk), :] = (m[:, : pairs // 2] + m[:, pairs // 2 :]).astype(BF)
        return c

    lax.fori_loop(0, ROWS // chunk, build_sel, 0)

    def build(p):
        pan = PANELS[p]
        src = feat.at[pan["J"]] if pan["kind"] == "f" else grad.at[pan["J"]]
        pick = self_f if pan["kind"] == "f" else sel

        def one(i, c):
            r0 = pl.multiple_of(i * 256, 256)
            v = jnp.dot(pick[pl.ds(r0, 256), :], src[...], preferred_element_type=F32)
            sb[pl.ds(pl.multiple_of(p * ROWS + r0, 256), 256), :] = v.astype(BF)
            return c

        lax.fori_loop(0, ROWS // 256, one, 0)
        own = pl.multiple_of(p * ROWS + me * CAP, CAP)
        rb[pl.ds(own, CAP), :] = sb[pl.ds(own, CAP), :]

    def push(p):
        def one(r, c):
            q, dev = plane_peer(r)
            pltpu.make_async_remote_copy(
                src_ref=sb.at[pl.ds(pl.multiple_of(p * ROWS + q * CAP, CAP), CAP), :],
                dst_ref=rb.at[pl.ds(pl.multiple_of(p * ROWS + me * CAP, CAP), CAP), :],
                send_sem=a_send.at[p],
                recv_sem=a_recv.at[p],
                device_id=dev,
                device_id_type=MESH,
            ).start()
            return c

        lax.fori_loop(1, E, one, 0)

    def wait_rows(ref, rows, sem):
        v = ref.at[pl.ds(0, rows), :]
        pltpu.make_async_copy(v, v, sem).wait()

    def compute(p):
        pan = PANELS[p]
        f0 = pan["first"]

        def one(i, c):
            k = i // 2
            h = i % 2
            a = rb[pl.ds(p * ROWS, ROWS), pl.ds(pl.multiple_of(h * 256, 256), 256)]
            b = rb[pl.ds(pl.multiple_of((f0 + k) * ROWS, ROWS), ROWS), :]
            v = lax.dot_general(a, b, (((0,), (0,)), ((), ())), preferred_element_type=F32)
            gram[pl.ds(pl.multiple_of((pan["ub"] + k) * W + h * 256, 256), 256), :] = v
            return c

        lax.fori_loop(0, 2 * (pan["J"] + 1), one, 0)

    def shard(pan, k, s):
        return gram[pl.ds(pl.multiple_of((pan["ub"] + k) * W + s * SUB, SUB), SUB), :]

    def seg(pan, t, k=0):
        return (t * UNITS + pan["ub"] + k) * SUB

    def height(pan):
        return (pan["J"] + 1) * SUB

    def remote(src, dst, ss, rs, dev):
        return pltpu.make_async_remote_copy(
            src_ref=src, dst_ref=dst, send_sem=ss, recv_sem=rs, device_id=dev, device_id_type=MESH
        )

    half = W // 2

    def ring(p, t, way):
        pan = PANELS[p]
        buf, ss, rs, dev = (
            (rsd, d_send, d_recv, down) if way == "d" else (rsu, u_send, u_recv, up)
        )
        n = height(pan)
        if t == 1:
            lanes = pl.ds(0 if way == "d" else half, half)
            src = st.at[pl.ds(pan["ub"] * SUB, n), lanes]
            dst = buf.at[pl.ds(seg(pan, 0), n), lanes]
        else:
            src = buf.at[pl.ds(seg(pan, t - 2), n), :]
            dst = buf.at[pl.ds(seg(pan, t - 1), n), :]
        return remote(src, dst, ss.at[p * 4 + t - 1], rs.at[p * 4 + t - 1], dev)

    def over_k(pan, fn):
        lax.fori_loop(0, pan["J"] + 1, lambda k, c: (fn(k), c)[1], 0)

    def step1(p):
        pan = PANELS[p]
        s = (z + 4) % N_Z

        def one(k):
            st[pl.ds(pl.multiple_of((pan["ub"] + k) * SUB, SUB), SUB), :] = shard(pan, k, s).astype(BF)

        over_k(pan, one)
        ring(p, 1, "d").start()
        ring(p, 1, "u").start()

    def step(p, t):
        pan = PANELS[p]
        for way in ("d", "u"):
            buf = rsd if way == "d" else rsu
            dist = 5 - t
            s = (z + N_Z - dist) % N_Z if way == "d" else (z + dist) % N_Z
            ring(p, t - 1, way).wait_recv()

            def one(k):
                r = pl.ds(pl.multiple_of(seg(pan, t - 2, k), SUB), SUB)
                own = shard(pan, k, s)
                if t == 2:
                    lo, hi = (slice(0, half), slice(half, W))
                    got, fresh = (lo, hi) if way == "d" else (hi, lo)
                    buf[r, got] = (buf[r, got].astype(F32) + own[:, got]).astype(BF)
                    buf[r, fresh] = own[:, fresh].astype(BF)
                else:
                    buf[r, :] = (buf[r, :].astype(F32) + own).astype(BF)

            over_k(pan, one)
            ring(p, t, way).start()

    def mirror_copy(p):
        pan = PANELS[p]
        rows = pl.ds(pan["ub"] * SUB, height(pan))
        return remote(ts.at[rows, :], tr.at[rows, :], t_send.at[p], t_recv.at[p], mirror)

    def finish(p):
        pan = PANELS[p]
        ring(p, 4, "d").wait_recv()
        ring(p, 4, "u").wait_recv()

        def one(k):
            r = pl.ds(pl.multiple_of(seg(pan, 3, k), SUB), SUB)
            v = shard(pan, k, z) + rsd[r, :].astype(F32) + rsu[r, :].astype(F32)
            ts[pl.ds(pl.multiple_of((pan["ub"] + k) * SUB, SUB), SUB), :] = v.astype(BF)

        over_k(pan, one)

        @pl.when(dp != z)
        def _():
            mirror_copy(p).start()

        @pl.when(dp == z)
        def _():
            def own(k):
                r = pl.ds(pl.multiple_of((pan["ub"] + k) * SUB, SUB), SUB)
                tr[r, :] = ts[r, :]

            over_k(pan, own)

    def tile_row(pan, b):
        return pan["tb"] * W + b * pan["J"] * SUB

    def spread(p):
        pan = PANELS[p]
        j = pan["J"]
        out = of if pan["kind"] == "f" else og

        @pl.when(dp != z)
        def _():
            mirror_copy(p).wait_recv()

        if j > 0:
            src_rows = pl.ds(pan["ub"] * SUB, j * SUB)
            dst_rows = pl.ds(pl.multiple_of(tile_row(pan, dp), SUB), j * SUB)

            def one(r, c):
                b = (dp + r) % N_DP
                lanes = pl.ds(pl.multiple_of((b // 2) * 128, 128), 128)
                remote(
                    tr.at[src_rows, lanes], tt.at[dst_rows, :], m_send.at[p], m_recv.at[p], (b, ex)
                ).start()
                return c

            lax.fori_loop(1, N_DP, one, 0)
            own_lanes = pl.ds(pl.multiple_of((dp // 2) * 128, 128), 128)
            tt[dst_rows, :] = tr[src_rows, own_lanes]
        for k in range(j + 1):
            v = tr[pl.ds((pan["ub"] + k) * SUB, SUB), :].astype(F32) * SCALE
            out[pl.ds(j * SUB, SUB), pl.ds(k * W, W)] = v

    def collect(p):
        pan = PANELS[p]
        j = pan["J"]
        if j == 0:
            return
        out = of if pan["kind"] == "f" else og
        wait_rows(tt, (N_DP - 1) * j * SUB, m_recv.at[p])
        off = (dp % 2) * SUB
        pick = lax.broadcasted_iota(jnp.int32, (SUB, 128), 1) == (
            lax.broadcasted_iota(jnp.int32, (SUB, 128), 0) + off
        )
        pick = jnp.where(pick, 1.0, 0.0).astype(BF)
        for k in range(j):
            parts = [tt[pl.ds(tile_row(pan, b) + k * SUB, SUB), :] for b in range(N_DP)]
            tiles = jnp.concatenate(parts, axis=0)
            v = lax.dot_general(pick, tiles, (((1,), (1,)), ((), ())), preferred_element_type=F32)
            out[pl.ds(k * SUB, SUB), pl.ds(j * W, W)] = v * SCALE

    def land(p):
        wait_rows(rb, (E - 1) * CAP, a_recv.at[p])

    build(0)
    build(1)
    pl.semaphore_wait(barrier, jnp.where(dp != z, E + 2, E + 1))

    push(0)
    push(1)
    for p in range(2, NP):
        build(p)
        if p < AHEAD:
            push(p)

    def front(p):
        land(p)
        if p + AHEAD < NP:
            push(p + AHEAD)
        compute(p)
        step1(p)

    for p in range(NP + 1):
        if p < NP:
            front(p)
        if p >= 1:
            step(p - 1, 3)
        if p < NP:
            step(p, 2)
        if p >= 1:
            step(p - 1, 4)
        if p >= 2:
            spread(p - 2)
        if p >= 1:
            finish(p - 1)
        if p >= 3:
            collect(p - 3)
    spread(NP - 1)
    collect(NP - 2)
    collect(NP - 1)

    for p in range(NP):
        wait_rows(sb, (E - 1) * CAP, a_send.at[p])
        for t in range(1, 5):
            ring(p, t, "d").wait_send()
            ring(p, t, "u").wait_send()

        @pl.when(dp != z)
        def _():
            mirror_copy(p).wait_send()

        j = PANELS[p]["J"]
        if j > 0:
            wait_rows(tt, (N_DP - 1) * j * SUB, m_send.at[p])


def per_device(features, expert_ids, gate_weights, out_grads):
    tokens, width = features.shape
    routes, hidden = out_grads.shape[1:]
    nf, ng = width // W, hidden // W
    feat = features.reshape(tokens, N_DP, nf, SUB).transpose(2, 0, 1, 3).reshape(nf, tokens, W)
    scaled = (out_grads.astype(F32) * gate_weights[:, :, None]).astype(BF)
    grad = (
        scaled.reshape(tokens, routes, N_DP, ng, SUB)
        .transpose(3, 1, 0, 2, 4)
        .reshape(ng, routes * tokens, W)
    )
    ids = expert_ids.T.reshape(1, routes * tokens)
    vm = pl.BlockSpec(memory_space=pltpu.VMEM)
    dma = pltpu.SemaphoreType.DMA
    of, og = pl.pallas_call(
        kernel,
        out_shape=(
            jax.ShapeDtypeStruct((nf * SUB, width), F32),
            jax.ShapeDtypeStruct((ng * SUB, hidden), F32),
        ),
        in_specs=[vm, vm, vm],
        out_specs=(vm, vm),
        scratch_shapes=[
            pltpu.VMEM((ROWS, routes * tokens), BF),
            pltpu.VMEM((ROWS, tokens), BF),
            pltpu.VMEM((NP * ROWS, W), BF),
            pltpu.VMEM((NP * ROWS, W), BF),
            pltpu.VMEM((UNITS * W, W), F32),
            pltpu.VMEM((4 * UNITS * SUB, W), BF),
            pltpu.VMEM((4 * UNITS * SUB, W), BF),
            pltpu.VMEM((UNITS * SUB, W), BF),
            pltpu.VMEM((UNITS * SUB, W), BF),
            pltpu.VMEM((UNITS * SUB, W), BF),
            pltpu.VMEM((TUNITS * W, 128), BF),
            dma((NP,)),
            dma((NP,)),
            dma((NP * 4,)),
            dma((NP * 4,)),
            dma((NP * 4,)),
            dma((NP * 4,)),
            dma((NP,)),
            dma((NP,)),
            dma((NP,)),
            dma((NP,)),
        ],
        compiler_params=pltpu.CompilerParams(
            collective_id=0, has_side_effects=True, vmem_limit_bytes=60 * 1024 * 1024
        ),
        cost_estimate=pl.CostEstimate(
            flops=9_000_000_000, bytes_accessed=8_000_000, transcendentals=0
        ),
    )(feat, grad, ids)
    of = of.reshape(nf * SUB, nf, N_DP, SUB).transpose(0, 2, 1, 3).reshape(1, nf * SUB, width)
    og = og.reshape(ng * SUB, ng, N_DP, SUB).transpose(0, 2, 1, 3).reshape(1, ng * SUB, hidden)
    return of, og


def solution(mesh):
    in_specs = (
        P(("dp", "expert"), None),
        P(("dp", "expert"), None),
        P(("dp", "expert"), None),
        P(("dp", "expert"), None, None),
    )
    out_specs = (P("expert", "dp", None), P("expert", "dp", None))
    return jax.shard_map(
        per_device, mesh=mesh, in_specs=in_specs, out_specs=out_specs, check_vma=False
    )
```

```python
import jax
import jax.numpy as jnp
from jax import lax
from jax.experimental import pallas as pl
from jax.experimental.pallas import tpu as pltpu
from jax.sharding import PartitionSpec as P

MESH = pl.DeviceIdType.MESH
BF = jnp.bfloat16
F32 = jnp.float32

N_DP = 8
N_Z = 8
N_Y = 4
E = 32
CAP = 32
ROWS = E * CAP
W = 512
SUB = 64
SCALE = 1.0 / 1024.0


def make_panels(nf, ng):
    panels = []
    ub = tb = 0
    for kind, count in (("f", nf), ("g", ng)):
        for j in range(count):
            panels.append(dict(kind=kind, J=j, ub=ub, tb=tb, first=len(panels) - j))
            ub += j + 1
            tb += j
    return panels, ub, tb


NF, NG = 4, 3
PANELS, UNITS, TUNITS = make_panels(NF, NG)
NP = len(PANELS)
AHEAD = 3


def make_order(first=8.0, every=12.5, hop=1.55, lag=2.5, mirror_lag=6.0, tile_lag=4.0):
    ready = {("land", p, 0): first + every * (p + 1) for p in range(NP)}
    link = now = 0.0
    order = []
    halves = dict.fromkeys(range(NP), 0)
    while ready:
        now = max(now, min(ready.values()))
        op = min(ready, key=lambda o: (ready[o], o[1], str(o[0]), o[2]))
        del ready[op]
        order.append(op)
        kind, p, h = op
        size = PANELS[p]["J"] + 1
        if kind == "land":
            now += 1.3 * size + 0.6
            for h in (0, 1):
                link = max(link, now) + 0.25 * hop * size
                ready[(2, p, h)] = link + lag
        elif kind == "sum":
            now += 0.15 * size + 0.1
            link = max(link, now) + 0.5 * hop * size
            halves[p] += 1
            if halves[p] == 2:
                ready[("out", p, 0)] = link + mirror_lag
        elif kind == "out":
            now += 0.2 * size + 0.3
            if size > 1:
                ready[("tile", p, 0)] = now + tile_lag + size
        elif kind == "tile":
            now += 0.5 * size
        else:
            now += 0.2 * size + 0.15
            link = max(link, now) + 0.5 * hop * size
            ready[(kind + 1 if kind < 4 else "sum", p, h)] = link + lag
    return order


def kernel(
    feats, grad0, grad1, gates, ids, of, og,
    feat, grad, sel, self_f, sb, rb, gram, rsd, rsu, st, ts, tr, tt,
    a_send, a_recv, d_send, d_recv, u_send, u_recv, t_send, t_recv, m_send, m_recv,
):
    dp = lax.axis_index("dp")
    ex = lax.axis_index("expert")
    z = ex // N_Y
    y = ex % N_Y
    me = dp * N_Y + y

    def plane_peer(r):
        q = (me + r) % E
        return q, (q // N_Y, z * N_Y + q % N_Y)

    down = (dp, ((z + N_Z - 1) % N_Z) * N_Y + y)
    up = (dp, ((z + 1) % N_Z) * N_Y + y)
    mirror = (z, dp * N_Y + y)

    barrier = pltpu.get_barrier_semaphore()

    def greet(r, c):
        pl.semaphore_signal(barrier, inc=1, device_id=plane_peer(r)[1], device_id_type=MESH)
        return c

    lax.fori_loop(1, E, greet, 0)
    pl.semaphore_signal(barrier, inc=1, device_id=down, device_id_type=MESH)
    pl.semaphore_signal(barrier, inc=1, device_id=up, device_id_type=MESH)

    @pl.when(dp != z)
    def _():
        pl.semaphore_signal(barrier, inc=1, device_id=mirror, device_id_type=MESH)

    pairs = ids.shape[1]
    idv = ids[...]
    hot = lax.broadcasted_iota(jnp.int32, (E, pairs), 0) == idv
    hot = jnp.where(hot, 1.0, 0.0)
    tri = lax.broadcasted_iota(jnp.int32, (pairs, pairs), 0) < lax.broadcasted_iota(
        jnp.int32, (pairs, pairs), 1
    )
    tri = jnp.where(tri, 1.0, 0.0).astype(BF)
    earlier = jnp.dot(hot.astype(BF), tri, preferred_element_type=F32)
    pos = jnp.sum(earlier * hot, axis=0, keepdims=True)
    target = idv * CAP + pos.astype(jnp.int32)
    chunk = 128

    def build_sel(i, c):
        r0 = pl.multiple_of(i * chunk, chunk)
        m = lax.broadcasted_iota(jnp.int32, (chunk, pairs), 0) + r0 == target
        m = jnp.where(m, 1.0, 0.0)
        sel[pl.ds(r0, chunk), :] = m.astype(BF)
        self_f[pl.ds(r0, chunk), :] = (m[:, : pairs // 2] + m[:, pairs // 2 :]).astype(BF)
        return c

    lax.fori_loop(0, ROWS // chunk, build_sel, 0)

    def gather_columns(pan, ref, b):
        count = NG if pan["kind"] == "g" else NF
        at = [((b + i) * count + pan["J"]) * SUB for i in (0, 1)]
        return [ref[:, pl.ds(a, SUB)] for a in at]

    def arrange(p):
        pan = PANELS[p]
        j = pan["J"]
        tokens = feats.shape[0]
        for m in range(N_DP // 2):
            lanes = slice(2 * SUB * m, 2 * SUB * (m + 1))
            if pan["kind"] == "f":
                feat[j, :, lanes] = jnp.concatenate(gather_columns(pan, feats, 2 * m), axis=1)
            else:
                for k, ref in enumerate((grad0, grad1)):
                    v = jnp.concatenate(gather_columns(pan, ref, 2 * m), axis=1)
                    v = (v.astype(F32) * gates[:, k : k + 1]).astype(BF)
                    grad[j, k * tokens : (k + 1) * tokens, lanes] = v

    def build(p):
        pan = PANELS[p]
        arrange(p)
        src = feat.at[pan["J"]] if pan["kind"] == "f" else grad.at[pan["J"]]
        pick = self_f if pan["kind"] == "f" else sel

        def one(i, c):
            r0 = pl.multiple_of(i * 256, 256)
            v = jnp.dot(pick[pl.ds(r0, 256), :], src[...], preferred_element_type=F32)
            sb[pl.ds(pl.multiple_of(p * ROWS + r0, 256), 256), :] = v.astype(BF)
            return c

        lax.fori_loop(0, ROWS // 256, one, 0)
        own = pl.multiple_of(p * ROWS + me * CAP, CAP)
        rb[pl.ds(own, CAP), :] = sb[pl.ds(own, CAP), :]

    def push(p):
        def one(r, c):
            q, dev = plane_peer(r)
            pltpu.make_async_remote_copy(
                src_ref=sb.at[pl.ds(pl.multiple_of(p * ROWS + q * CAP, CAP), CAP), :],
                dst_ref=rb.at[pl.ds(pl.multiple_of(p * ROWS + me * CAP, CAP), CAP), :],
                send_sem=a_send.at[p],
                recv_sem=a_recv.at[p],
                device_id=dev,
                device_id_type=MESH,
            ).start()
            return c

        lax.fori_loop(1, E, one, 0)

    def wait_rows(ref, rows, sem):
        v = ref.at[pl.ds(0, rows), :]
        pltpu.make_async_copy(v, v, sem).wait()

    def compute(p):
        pan = PANELS[p]
        f0 = pan["first"]

        def one(i, c):
            k = i // 2
            h = i % 2
            a = rb[pl.ds(p * ROWS, ROWS), pl.ds(pl.multiple_of(h * 256, 256), 256)]
            b = rb[pl.ds(pl.multiple_of((f0 + k) * ROWS, ROWS), ROWS), :]
            v = lax.dot_general(a, b, (((0,), (0,)), ((), ())), preferred_element_type=F32)
            gram[pl.ds(pl.multiple_of((pan["ub"] + k) * W + h * 256, 256), 256), :] = v
            return c

        lax.fori_loop(0, 2 * (pan["J"] + 1), one, 0)

    def shard(pan, k, s, lanes=slice(None)):
        return gram[pl.ds(pl.multiple_of((pan["ub"] + k) * W + s * SUB, SUB), SUB), lanes]

    def seg(pan, t, k=0):
        return (t * UNITS + pan["ub"] + k) * SUB

    def height(pan):
        return (pan["J"] + 1) * SUB

    def remote(src, dst, ss, rs, dev):
        return pltpu.make_async_remote_copy(
            src_ref=src, dst_ref=dst, send_sem=ss, recv_sem=rs, device_id=dev, device_id_type=MESH
        )

    half = W // 2

    def half_lanes(h):
        return pl.ds(h * half, half)

    def ring(p, t, way, h):
        pan = PANELS[p]
        buf, ss, rs, dev = (
            (rsd, d_send, d_recv, down) if way == "d" else (rsu, u_send, u_recv, up)
        )
        n = height(pan)
        lanes = half_lanes(h)
        if t == 1:
            src = st.at[pl.ds(pan["ub"] * SUB, n), lanes]
        else:
            src = buf.at[pl.ds(seg(pan, t - 2), n), lanes]
        dst = buf.at[pl.ds(seg(pan, t - 1), n), lanes]
        i = (p * 4 + t - 1) * 2 + h
        return remote(src, dst, ss.at[i], rs.at[i], dev)

    def over_k(pan, fn):
        lax.fori_loop(0, pan["J"] + 1, lambda k, c: (fn(k), c)[1], 0)

    def far(h):
        return "d" if h == 0 else "u"

    def step1(p):
        pan = PANELS[p]
        s = (z + 4) % N_Z

        def one(k):
            st[pl.ds(pl.multiple_of((pan["ub"] + k) * SUB, SUB), SUB), :] = shard(pan, k, s).astype(BF)

        over_k(pan, one)
        for h in (0, 1):
            ring(p, 1, far(h), h).start()

    def step(p, t, h):
        pan = PANELS[p]
        lanes = half_lanes(h)
        order = ("d", "u") if far(h) == "u" else ("u", "d")
        for way in order:
            buf = rsd if way == "d" else rsu
            dist = 5 - t
            s = (z + N_Z - dist) % N_Z if way == "d" else (z + dist) % N_Z
            fresh = t == 2 and way != far(h)
            if not fresh:
                ring(p, t - 1, way, h).wait_recv()

            def one(k):
                r = pl.ds(pl.multiple_of(seg(pan, t - 2, k), SUB), SUB)
                own = shard(pan, k, s, lanes)
                if not fresh:
                    own = own + buf[r, lanes].astype(F32)
                buf[r, lanes] = own.astype(BF)

            over_k(pan, one)
            ring(p, t, way, h).start()

    def mirror_copy(p, h):
        pan = PANELS[p]
        rows = pl.ds(pan["ub"] * SUB, height(pan))
        i = p * 2 + h
        lanes = half_lanes(h)
        return remote(ts.at[rows, lanes], tr.at[rows, lanes], t_send.at[i], t_recv.at[i], mirror)

    def finish(p, h):
        pan = PANELS[p]
        lanes = half_lanes(h)
        ring(p, 4, "d", h).wait_recv()
        ring(p, 4, "u", h).wait_recv()

        def one(k):
            r = pl.ds(pl.multiple_of(seg(pan, 3, k), SUB), SUB)
            v = shard(pan, k, z, lanes) + rsd[r, lanes].astype(F32) + rsu[r, lanes].astype(F32)
            ts[pl.ds(pl.multiple_of((pan["ub"] + k) * SUB, SUB), SUB), lanes] = v.astype(BF)

        over_k(pan, one)

        @pl.when(dp != z)
        def _():
            mirror_copy(p, h).start()

        @pl.when(dp == z)
        def _():
            def own(k):
                r = pl.ds(pl.multiple_of((pan["ub"] + k) * SUB, SUB), SUB)
                tr[r, lanes] = ts[r, lanes]

            over_k(pan, own)

    def put(pan, row, col, v):
        out, count = (of, NF) if pan["kind"] == "f" else (og, NG)
        v = v * SCALE
        for b in range(N_DP):
            c = (b * count + col) * SUB
            out[0, pl.ds(row * SUB, SUB), pl.ds(c, SUB)] = v[:, b * SUB : (b + 1) * SUB]

    def tile_row(pan, b):
        return pan["tb"] * W + b * pan["J"] * SUB

    def spread(p):
        pan = PANELS[p]
        j = pan["J"]

        @pl.when(dp != z)
        def _():
            mirror_copy(p, 0).wait_recv()
            mirror_copy(p, 1).wait_recv()

        if j > 0:
            src_rows = pl.ds(pan["ub"] * SUB, j * SUB)
            dst_rows = pl.ds(pl.multiple_of(tile_row(pan, dp), SUB), j * SUB)

            def one(r, c):
                b = (dp + r) % N_DP
                lanes = pl.ds(pl.multiple_of((b // 2) * 128, 128), 128)
                remote(
                    tr.at[src_rows, lanes], tt.at[dst_rows, :], m_send.at[p], m_recv.at[p], (b, ex)
                ).start()
                return c

            lax.fori_loop(1, N_DP, one, 0)
            own_lanes = pl.ds(pl.multiple_of((dp // 2) * 128, 128), 128)
            tt[dst_rows, :] = tr[src_rows, own_lanes]
        for k in range(j + 1):
            put(pan, j, k, tr[pl.ds((pan["ub"] + k) * SUB, SUB), :].astype(F32))

    def collect(p):
        pan = PANELS[p]
        j = pan["J"]
        if j == 0:
            return
        wait_rows(tt, (N_DP - 1) * j * SUB, m_recv.at[p])
        off = (dp % 2) * SUB
        pick = lax.broadcasted_iota(jnp.int32, (SUB, 128), 1) == (
            lax.broadcasted_iota(jnp.int32, (SUB, 128), 0) + off
        )
        pick = jnp.where(pick, 1.0, 0.0).astype(BF)
        for k in range(j):
            parts = [tt[pl.ds(tile_row(pan, b) + k * SUB, SUB), :] for b in range(N_DP)]
            tiles = jnp.concatenate(parts, axis=0)
            v = lax.dot_general(pick, tiles, (((1,), (1,)), ((), ())), preferred_element_type=F32)
            put(pan, k, j, v)

    def land(p):
        wait_rows(rb, (E - 1) * CAP, a_recv.at[p])

    build(0)
    build(1)
    pl.semaphore_wait(barrier, jnp.where(dp != z, E + 2, E + 1))

    push(0)
    push(1)
    for p in range(2, NP):
        build(p)
        if p < AHEAD:
            push(p)

    def front(p):
        land(p)
        if p + AHEAD < NP:
            push(p + AHEAD)
        compute(p)
        step1(p)

    for kind, p, h in make_order():
        if kind == "land":
            front(p)
        elif kind == "sum":
            finish(p, h)
        elif kind == "out":
            spread(p)
        elif kind == "tile":
            collect(p)
        else:
            step(p, kind, h)

    for p in range(NP):
        wait_rows(sb, (E - 1) * CAP, a_send.at[p])
        for h in (0, 1):
            ring(p, 1, far(h), h).wait_send()
            for t in (2, 3, 4):
                ring(p, t, "d", h).wait_send()
                ring(p, t, "u", h).wait_send()

        @pl.when(dp != z)
        def _():
            mirror_copy(p, 0).wait_send()
            mirror_copy(p, 1).wait_send()

        j = PANELS[p]["J"]
        if j > 0:
            wait_rows(tt, (N_DP - 1) * j * SUB, m_send.at[p])


def per_device(features, expert_ids, gate_weights, out_grads):
    tokens, width = features.shape
    routes, hidden = out_grads.shape[1:]
    nf, ng = width // W, hidden // W
    ids = expert_ids.T.reshape(1, routes * tokens)
    vm = pl.BlockSpec(memory_space=pltpu.VMEM)
    dma = pltpu.SemaphoreType.DMA
    of, og = pl.pallas_call(
        kernel,
        out_shape=(
            jax.ShapeDtypeStruct((1, nf * SUB, width), F32),
            jax.ShapeDtypeStruct((1, ng * SUB, hidden), F32),
        ),
        in_specs=[vm] * 5,
        out_specs=(vm, vm),
        scratch_shapes=[
            pltpu.VMEM((nf, tokens, W), BF),
            pltpu.VMEM((ng, routes * tokens, W), BF),
            pltpu.VMEM((ROWS, routes * tokens), BF),
            pltpu.VMEM((ROWS, tokens), BF),
            pltpu.VMEM((NP * ROWS, W), BF),
            pltpu.VMEM((NP * ROWS, W), BF),
            pltpu.VMEM((UNITS * W, W), F32),
            pltpu.VMEM((4 * UNITS * SUB, W), BF),
            pltpu.VMEM((4 * UNITS * SUB, W), BF),
            pltpu.VMEM((UNITS * SUB, W), BF),
            pltpu.VMEM((UNITS * SUB, W), BF),
            pltpu.VMEM((UNITS * SUB, W), BF),
            pltpu.VMEM((TUNITS * W, 128), BF),
            dma((NP,)),
            dma((NP,)),
            dma((NP * 8,)),
            dma((NP * 8,)),
            dma((NP * 8,)),
            dma((NP * 8,)),
            dma((NP * 2,)),
            dma((NP * 2,)),
            dma((NP,)),
            dma((NP,)),
        ],
        compiler_params=pltpu.CompilerParams(
            collective_id=0, has_side_effects=True, vmem_limit_bytes=60 * 1024 * 1024
        ),
        cost_estimate=pl.CostEstimate(
            flops=9_000_000_000, bytes_accessed=8_000_000, transcendentals=0
        ),
    )(features, out_grads[:, 0, :], out_grads[:, 1, :], gate_weights, ids)
    return of, og


def solution(mesh):
    in_specs = (
        P(("dp", "expert"), None),
        P(("dp", "expert"), None),
        P(("dp", "expert"), None),
        P(("dp", "expert"), None, None),
    )
    out_specs = (P("expert", "dp", None), P("expert", "dp", None))
    return jax.shard_map(
        per_device, mesh=mesh, in_specs=in_specs, out_specs=out_specs, check_vma=False
    )
```

```python
import jax
import jax.numpy as jnp
from jax import lax
from jax.experimental import pallas as pl
from jax.experimental.pallas import tpu as pltpu
from jax.sharding import PartitionSpec as P

MESH = pl.DeviceIdType.MESH
BF = jnp.bfloat16
F32 = jnp.float32

N_DP = 8
N_Z = 8
N_Y = 4
E = 32
CAP = 32
ROWS = E * CAP
W = 512
SUB = 64
SCALE = 1.0 / 1024.0


PR, PC = 32, 128
HALF = N_DP // 2
HR = HALF * PR


def make_panels(nf, ng):
    panels = []
    ub = tb = 0
    for kind, count in (("f", nf), ("g", ng)):
        for j in range(count):
            panels.append(dict(kind=kind, J=j, ub=ub, tb=tb, first=len(panels) - j))
            ub += j + 1
            tb += j
    return panels, ub, tb


NF, NG = 4, 3
PANELS, UNITS, TUNITS = make_panels(NF, NG)
NP = len(PANELS)
AHEAD = 3


def make_order(first=8.0, every=12.5, hop=1.6, lag=2.5, move_lag=4.0):
    ready = {("land", p, 0): first + every * (p + 1) for p in range(NP)}
    link = now = 0.0
    order = []
    halves = dict.fromkeys(range(NP), 0)
    while ready:
        now = max(now, min(ready.values()))
        op = min(ready, key=lambda o: (ready[o], o[1], str(o[0]), o[2]))
        del ready[op]
        order.append(op)
        kind, p, h = op
        size = PANELS[p]["J"] + 1
        if kind == "land":
            now += 1.3 * size + 3.0
            for h in (0, 1):
                link = max(link, now) + 0.25 * hop * size
                ready[(2, p, h)] = link + lag
        elif kind == "sum":
            now += 0.3 * size + 0.3
            ready[("turn", p, 0)] = now + 0.5 * size + move_lag
        elif kind == "turn":
            now += 0.3
            link = max(link, now) + hop * size
            ready[("out", p, 0)] = link + move_lag
        elif kind == "out":
            now += 0.3 * size + 0.3
            if size > 1:
                ready[("tile", p, 0)] = now + move_lag + size
        elif kind == "tile":
            now += 0.5 * size
        else:
            now += 0.2 * size + 0.15
            link = max(link, now) + 0.5 * hop * size
            if kind < 4:
                ready[(kind + 1, p, h)] = link + lag
            else:
                halves[p] += 1
                if halves[p] == 2:
                    ready[("sum", p, 0)] = link + lag
    return order


def kernel(
    feats, grad0, grad1, gates, ids, of, og,
    feat, grad, sel, self_f, sb, rb, gram, rsd, rsu, st, ts, tx, tr, tt,
    a_send, a_recv, d_send, d_recv, u_send, u_recv,
    x_send, x_recv, z_send, z_recv, m_send, m_recv,
):
    dp = lax.axis_index("dp")
    ex = lax.axis_index("expert")
    z = ex // N_Y
    y = ex % N_Y
    me = dp * N_Y + y

    def plane_peer(r):
        q = (me + r) % E
        return q, (q // N_Y, z * N_Y + q % N_Y)

    def line_peer(r):
        q = (z + r) % N_Z
        return q, (dp, q * N_Y + y)

    down = (dp, ((z + N_Z - 1) % N_Z) * N_Y + y)
    up = (dp, ((z + 1) % N_Z) * N_Y + y)

    barrier = pltpu.get_barrier_semaphore()

    def greet(r, c):
        pl.semaphore_signal(barrier, inc=1, device_id=plane_peer(r)[1], device_id_type=MESH)
        return c

    def greet_line(r, c):
        pl.semaphore_signal(barrier, inc=1, device_id=line_peer(r)[1], device_id_type=MESH)
        return c

    lax.fori_loop(1, E, greet, 0)
    lax.fori_loop(1, N_Z, greet_line, 0)

    pairs = ids.shape[1]
    idv = ids[...]
    hot = lax.broadcasted_iota(jnp.int32, (E, pairs), 0) == idv
    hot = jnp.where(hot, 1.0, 0.0)
    tri = lax.broadcasted_iota(jnp.int32, (pairs, pairs), 0) < lax.broadcasted_iota(
        jnp.int32, (pairs, pairs), 1
    )
    tri = jnp.where(tri, 1.0, 0.0).astype(BF)
    earlier = jnp.dot(hot.astype(BF), tri, preferred_element_type=F32)
    pos = jnp.sum(earlier * hot, axis=0, keepdims=True)
    target = idv * CAP + pos.astype(jnp.int32)
    chunk = 128

    def build_sel(i, c):
        r0 = pl.multiple_of(i * chunk, chunk)
        m = lax.broadcasted_iota(jnp.int32, (chunk, pairs), 0) + r0 == target
        m = jnp.where(m, 1.0, 0.0)
        sel[pl.ds(r0, chunk), :] = m.astype(BF)
        self_f[pl.ds(r0, chunk), :] = (m[:, : pairs // 2] + m[:, pairs // 2 :]).astype(BF)
        return c

    lax.fori_loop(0, ROWS // chunk, build_sel, 0)

    def gather_columns(pan, ref, b):
        count = NG if pan["kind"] == "g" else NF
        at = [((b + i) * count + pan["J"]) * SUB for i in (0, 1)]
        return [ref[:, pl.ds(a, SUB)] for a in at]

    def arrange(p):
        pan = PANELS[p]
        j = pan["J"]
        tokens = feats.shape[0]
        for m in range(N_DP // 2):
            lanes = slice(2 * SUB * m, 2 * SUB * (m + 1))
            if pan["kind"] == "f":
                feat[j, :, lanes] = jnp.concatenate(gather_columns(pan, feats, 2 * m), axis=1)
            else:
                for k, ref in enumerate((grad0, grad1)):
                    v = jnp.concatenate(gather_columns(pan, ref, 2 * m), axis=1)
                    v = (v.astype(F32) * gates[:, k : k + 1]).astype(BF)
                    grad[j, k * tokens : (k + 1) * tokens, lanes] = v

    def build(p):
        pan = PANELS[p]
        arrange(p)
        src = feat.at[pan["J"]] if pan["kind"] == "f" else grad.at[pan["J"]]
        pick = self_f if pan["kind"] == "f" else sel

        def one(i, c):
            r0 = pl.multiple_of(i * 256, 256)
            v = jnp.dot(pick[pl.ds(r0, 256), :], src[...], preferred_element_type=F32)
            sb[pl.ds(pl.multiple_of(p * ROWS + r0, 256), 256), :] = v.astype(BF)
            return c

        lax.fori_loop(0, ROWS // 256, one, 0)
        own = pl.multiple_of(p * ROWS + me * CAP, CAP)
        rb[pl.ds(own, CAP), :] = sb[pl.ds(own, CAP), :]

    def push(p):
        def one(r, c):
            q, dev = plane_peer(r)
            pltpu.make_async_remote_copy(
                src_ref=sb.at[pl.ds(pl.multiple_of(p * ROWS + q * CAP, CAP), CAP), :],
                dst_ref=rb.at[pl.ds(pl.multiple_of(p * ROWS + me * CAP, CAP), CAP), :],
                send_sem=a_send.at[p],
                recv_sem=a_recv.at[p],
                device_id=dev,
                device_id_type=MESH,
            ).start()
            return c

        lax.fori_loop(1, E, one, 0)

    def wait_rows(ref, rows, sem):
        v = ref.at[pl.ds(0, rows), :]
        pltpu.make_async_copy(v, v, sem).wait()

    def compute(p):
        pan = PANELS[p]
        f0 = pan["first"]

        def one(i, c):
            k = i // 2
            h = i % 2
            a = rb[pl.ds(p * ROWS, ROWS), pl.ds(pl.multiple_of(h * 256, 256), 256)]
            b = rb[pl.ds(pl.multiple_of((f0 + k) * ROWS, ROWS), ROWS), :]
            v = lax.dot_general(a, b, (((0,), (0,)), ((), ())), preferred_element_type=F32)
            gram[pl.ds(pl.multiple_of((pan["ub"] + k) * W + h * 256, 256), 256), :] = v
            return c

        lax.fori_loop(0, 2 * (pan["J"] + 1), one, 0)

    def piece(pan, k, s, b):
        r = (pan["ub"] + k) * W + b * SUB + (s % 2) * PR
        lanes = pl.ds(pl.multiple_of((s // 2) * PC, PC), PC)
        return gram[pl.ds(pl.multiple_of(r, PR), PR), lanes]

    def seg(pan, t, h=0, k=0, b=0):
        return ((t * UNITS + pan["ub"]) * 2 + h * (pan["J"] + 1) + k) * HR + b * PR

    def height(pan):
        return (pan["J"] + 1) * HR

    def remote(src, dst, ss, rs, dev):
        return pltpu.make_async_remote_copy(
            src_ref=src, dst_ref=dst, send_sem=ss, recv_sem=rs, device_id=dev, device_id_type=MESH
        )

    def ring(p, t, way, h):
        pan = PANELS[p]
        buf, ss, rs, dev = (
            (rsd, d_send, d_recv, down) if way == "d" else (rsu, u_send, u_recv, up)
        )
        n = height(pan)
        if t == 1:
            src = st.at[pl.ds(seg(pan, 0, h), n), :]
        else:
            src = buf.at[pl.ds(seg(pan, t - 2, h), n), :]
        dst = buf.at[pl.ds(seg(pan, t - 1, h), n), :]
        i = (p * 4 + t - 1) * 2 + h
        return remote(src, dst, ss.at[i], rs.at[i], dev)

    def over_k(pan, fn):
        lax.fori_loop(0, pan["J"] + 1, lambda k, c: (fn(k), c)[1], 0)

    def far(h):
        return "d" if h == 0 else "u"

    def ring_rows(pan, t, h, k, b):
        return pl.ds(pl.multiple_of(seg(pan, t, h, k, b), PR), PR)

    def step1(p):
        pan = PANELS[p]
        s = (z + 4) % N_Z
        for h in (0, 1):

            def one(k):
                for b in range(HALF):
                    st[ring_rows(pan, 0, h, k, b), :] = piece(pan, k, s, h * HALF + b).astype(BF)

            over_k(pan, one)
            ring(p, 1, far(h), h).start()

    def step(p, t, h):
        pan = PANELS[p]
        order = ("d", "u") if far(h) == "u" else ("u", "d")
        for way in order:
            buf = rsd if way == "d" else rsu
            dist = 5 - t
            s = (z + N_Z - dist) % N_Z if way == "d" else (z + dist) % N_Z
            fresh = t == 2 and way != far(h)
            if not fresh:
                ring(p, t - 1, way, h).wait_recv()

            def one(k):
                for b in range(HALF):
                    r = ring_rows(pan, t - 2, h, k, b)
                    own = piece(pan, k, s, h * HALF + b)
                    if not fresh:
                        own = own + buf[r, :].astype(F32)
                    buf[r, :] = own.astype(BF)

            over_k(pan, one)
            ring(p, t, way, h).start()

    def slot(pan, q, k=0):
        return pan["ub"] * N_DP + q * (pan["J"] + 1) + k

    def slots(pan, q):
        return pl.ds(slot(pan, q), pan["J"] + 1)

    def place(pan, q):
        return (
            pl.ds(pan["ub"], pan["J"] + 1),
            pl.ds(pl.multiple_of((q % 2) * PR, PR), PR),
            pl.ds(pl.multiple_of((q // 2) * PC, PC), PC),
        )

    def finish(p):
        pan = PANELS[p]
        for h in (0, 1):
            ring(p, 4, "d", h).wait_recv()
            ring(p, 4, "u", h).wait_recv()

            def one(k):
                for b in range(HALF):
                    r = ring_rows(pan, 3, h, k, b)
                    v = piece(pan, k, z, h * HALF + b) + rsd[r, :].astype(F32) + rsu[r, :].astype(F32)
                    ts[slot(pan, h * HALF + b, k)] = v.astype(BF)

            over_k(pan, one)

        def one_peer(r, c):
            b = (dp + r) % N_DP
            remote(
                ts.at[slots(pan, b)], tx.at[slots(pan, dp)], x_send.at[p], x_recv.at[p], (b, ex)
            ).start()
            return c

        lax.fori_loop(1, N_DP, one_peer, 0)
        tx[slots(pan, dp)] = ts[slots(pan, dp)]

    def turn(p):
        pan = PANELS[p]
        wait_slots(pan, x_recv.at[p])

        def one_peer(r, c):
            q, dev = line_peer(r)
            remote(
                tx.at[slots(pan, q)], tr.at[place(pan, z)], z_send.at[p], z_recv.at[p], dev
            ).start()
            return c

        lax.fori_loop(1, N_Z, one_peer, 0)
        tr[place(pan, z)] = tx[slots(pan, z)]

    def wait_slots(pan, sem):
        v = ts.at[pl.ds(0, (N_DP - 1) * (pan["J"] + 1))]
        pltpu.make_async_copy(v, v, sem).wait()

    def put(pan, row, col, v):
        out, count = (of, NF) if pan["kind"] == "f" else (og, NG)
        v = v * SCALE
        for b in range(N_DP):
            c = (b * count + col) * SUB
            out[0, pl.ds(row * SUB, SUB), pl.ds(c, SUB)] = v[:, b * SUB : (b + 1) * SUB]

    def tile_slot(pan, b):
        return pan["tb"] * N_DP + b * pan["J"]

    def wait_tiles(j, sem):
        v = tt.at[pl.ds(0, (N_DP - 1) * j)]
        pltpu.make_async_copy(v, v, sem).wait()

    def spread(p):
        pan = PANELS[p]
        j = pan["J"]
        wait_slots(pan, z_recv.at[p])
        if j > 0:
            mine = pl.ds(pan["ub"], j)
            dst = pl.ds(tile_slot(pan, dp), j)

            def one(r, c):
                b = (dp + r) % N_DP
                lanes = pl.ds(pl.multiple_of((b // 2) * 128, 128), 128)
                remote(
                    tr.at[mine, :, lanes], tt.at[dst], m_send.at[p], m_recv.at[p], (b, ex)
                ).start()
                return c

            lax.fori_loop(1, N_DP, one, 0)
            own_lanes = pl.ds(pl.multiple_of((dp // 2) * 128, 128), 128)
            tt[dst] = tr[mine, :, own_lanes]
        for k in range(j + 1):
            put(pan, j, k, tr[pan["ub"] + k].astype(F32))

    def collect(p):
        pan = PANELS[p]
        j = pan["J"]
        if j == 0:
            return
        wait_tiles(j, m_recv.at[p])
        off = (dp % 2) * SUB
        pick = lax.broadcasted_iota(jnp.int32, (SUB, 128), 1) == (
            lax.broadcasted_iota(jnp.int32, (SUB, 128), 0) + off
        )
        pick = jnp.where(pick, 1.0, 0.0).astype(BF)
        for k in range(j):
            parts = [tt[tile_slot(pan, b) + k] for b in range(N_DP)]
            tiles = jnp.concatenate(parts, axis=0)
            v = lax.dot_general(pick, tiles, (((1,), (1,)), ((), ())), preferred_element_type=F32)
            put(pan, k, j, v)

    def land(p):
        wait_rows(rb, (E - 1) * CAP, a_recv.at[p])

    build(0)
    pl.semaphore_wait(barrier, E - 1 + N_Z - 1)
    push(0)
    for p in range(1, AHEAD):
        build(p)
        push(p)

    def front(p):
        land(p)
        if p + AHEAD < NP:
            build(p + AHEAD)
            push(p + AHEAD)
        compute(p)
        step1(p)

    for kind, p, h in make_order():
        if kind == "land":
            front(p)
        elif kind == "sum":
            finish(p)
        elif kind == "turn":
            turn(p)
        elif kind == "out":
            spread(p)
        elif kind == "tile":
            collect(p)
        else:
            step(p, kind, h)

    for p in range(NP):
        wait_rows(sb, (E - 1) * CAP, a_send.at[p])
        for h in (0, 1):
            ring(p, 1, far(h), h).wait_send()
            for t in (2, 3, 4):
                ring(p, t, "d", h).wait_send()
                ring(p, t, "u", h).wait_send()
        wait_slots(PANELS[p], x_send.at[p])
        wait_slots(PANELS[p], z_send.at[p])
        j = PANELS[p]["J"]
        if j > 0:
            wait_tiles(j, m_send.at[p])


def per_device(features, expert_ids, gate_weights, out_grads):
    tokens, width = features.shape
    routes, hidden = out_grads.shape[1:]
    nf, ng = width // W, hidden // W
    ids = expert_ids.T.reshape(1, routes * tokens)
    vm = pl.BlockSpec(memory_space=pltpu.VMEM)
    dma = pltpu.SemaphoreType.DMA
    of, og = pl.pallas_call(
        kernel,
        out_shape=(
            jax.ShapeDtypeStruct((1, nf * SUB, width), F32),
            jax.ShapeDtypeStruct((1, ng * SUB, hidden), F32),
        ),
        in_specs=[vm] * 5,
        out_specs=(vm, vm),
        scratch_shapes=[
            pltpu.VMEM((nf, tokens, W), BF),
            pltpu.VMEM((ng, routes * tokens, W), BF),
            pltpu.VMEM((ROWS, routes * tokens), BF),
            pltpu.VMEM((ROWS, tokens), BF),
            pltpu.VMEM((NP * ROWS, W), BF),
            pltpu.VMEM((NP * ROWS, W), BF),
            pltpu.VMEM((UNITS * W, W), F32),
            pltpu.VMEM((4 * UNITS * 2 * HR, PC), BF),
            pltpu.VMEM((4 * UNITS * 2 * HR, PC), BF),
            pltpu.VMEM((UNITS * 2 * HR, PC), BF),
            pltpu.VMEM((UNITS * N_DP, PR, PC), BF),
            pltpu.VMEM((UNITS * N_DP, PR, PC), BF),
            pltpu.VMEM((UNITS, SUB, W), BF),
            pltpu.VMEM((TUNITS * N_DP, SUB, 128), BF),
            dma((NP,)),
            dma((NP,)),
            dma((NP * 8,)),
            dma((NP * 8,)),
            dma((NP * 8,)),
            dma((NP * 8,)),
            dma((NP,)),
            dma((NP,)),
            dma((NP,)),
            dma((NP,)),
            dma((NP,)),
            dma((NP,)),
        ],
        compiler_params=pltpu.CompilerParams(
            collective_id=0, has_side_effects=True, vmem_limit_bytes=60 * 1024 * 1024
        ),
        cost_estimate=pl.CostEstimate(
            flops=9_000_000_000, bytes_accessed=8_000_000, transcendentals=0
        ),
    )(features, out_grads[:, 0, :], out_grads[:, 1, :], gate_weights, ids)
    return of, og


def solution(mesh):
    in_specs = (
        P(("dp", "expert"), None),
        P(("dp", "expert"), None),
        P(("dp", "expert"), None),
        P(("dp", "expert"), None, None),
    )
    out_specs = (P("expert", "dp", None), P("expert", "dp", None))
    return jax.shard_map(
        per_device, mesh=mesh, in_specs=in_specs, out_specs=out_specs, check_vma=False
    )
```

```python
import jax
import jax.numpy as jnp
from jax import lax
from jax.experimental import pallas as pl
from jax.experimental.pallas import tpu as pltpu
from jax.sharding import PartitionSpec as P

MESH = pl.DeviceIdType.MESH
BF = jnp.bfloat16
F32 = jnp.float32

N_DP = 8
N_Z = 8
N_Y = 4
E = 32
CAP = 32
ROWS = E * CAP
W = 512
SUB = 64
SCALE = 1.0 / 1024.0


PR, PC = 32, 128
HALF = N_DP // 2
DIAG = 3


def half_pieces(j):
    return j * HALF + DIAG


def make_panels(nf, ng):
    panels = []
    ub = tb = rb = 0
    for kind, count in (("f", nf), ("g", ng)):
        for j in range(count):
            panels.append(dict(kind=kind, J=j, ub=ub, tb=tb, rb=rb, first=len(panels) - j))
            ub += j + 1
            tb += j
            rb += 2 * half_pieces(j)
    return panels, ub, tb, rb


NF, NG = 4, 3
PANELS, UNITS, TUNITS, PIECES = make_panels(NF, NG)
NP = len(PANELS)
AHEAD = 3


def make_order(first=8.0, every=12.5, hop=1.6, lag=2.5, move_lag=4.0):
    ready = {("land", p, 0): first + every * (p + 1) for p in range(NP)}
    link = now = 0.0
    order = []
    halves = dict.fromkeys(range(NP), 0)
    while ready:
        now = max(now, min(ready.values()))
        op = min(ready, key=lambda o: (ready[o], o[1], str(o[0]), o[2]))
        del ready[op]
        order.append(op)
        kind, p, h = op
        size = PANELS[p]["J"] + 1
        ring_size = PANELS[p]["J"] + 0.75
        if kind == "land":
            now += 1.3 * size + 3.0
            for h in (0, 1):
                link = max(link, now) + 0.25 * hop * ring_size
                ready[(2, p, h)] = link + lag
        elif kind == "sum":
            now += 0.3 * size + 0.3
            ready[("turn", p, 0)] = now + 0.5 * size + move_lag
        elif kind == "turn":
            now += 0.3
            link = max(link, now) + hop * size
            ready[("out", p, 0)] = link + move_lag
        elif kind == "out":
            now += 0.3 * size + 0.3
            ready[("tile", p, 0)] = now + move_lag + size
        elif kind == "tile":
            now += 0.5 * size
        else:
            now += 0.2 * size + 0.15
            link = max(link, now) + 0.5 * hop * ring_size
            if kind < 4:
                ready[(kind + 1, p, h)] = link + lag
            else:
                halves[p] += 1
                if halves[p] == 2:
                    ready[("sum", p, 0)] = link + lag
    return order


def kernel(
    feats, grads, gates, ids, of, og,
    feat, grad, sel, self_f, sb, rb, gram, rsd, rsu, st, ts, tx, tr, tt, td,
    a_send, a_recv, d_send, d_recv, u_send, u_recv,
    x_send, x_recv, z_send, z_recv, m_send, m_recv, e_send, e_recv,
):
    dp = lax.axis_index("dp")
    ex = lax.axis_index("expert")
    z = ex // N_Y
    y = ex % N_Y
    me = dp * N_Y + y

    def plane_peer(r):
        q = (me + r) % E
        return q, (q // N_Y, z * N_Y + q % N_Y)

    def line_peer(r):
        q = (z + r) % N_Z
        return q, (dp, q * N_Y + y)

    down = (dp, ((z + N_Z - 1) % N_Z) * N_Y + y)
    up = (dp, ((z + 1) % N_Z) * N_Y + y)

    barrier = pltpu.get_barrier_semaphore()

    def greet(r, c):
        pl.semaphore_signal(barrier, inc=1, device_id=plane_peer(r)[1], device_id_type=MESH)
        return c

    def greet_line(r, c):
        pl.semaphore_signal(barrier, inc=1, device_id=line_peer(r)[1], device_id_type=MESH)
        return c

    lax.fori_loop(1, E, greet, 0)
    lax.fori_loop(1, N_Z, greet_line, 0)

    tokens = feats.shape[0]
    pairs = grads.shape[0]
    idv = jnp.concatenate([ids[k : k + 1, :] for k in range(pairs // tokens)], axis=1)

    def iota(shape, dim):
        return lax.broadcasted_iota(jnp.int32, shape, dim)

    def ones_where(m):
        return jnp.where(m, 1.0, 0.0)

    hot = ones_where(iota((E, pairs), 0) == idv)
    tri = ones_where(iota((pairs, pairs), 0) < iota((pairs, pairs), 1)).astype(BF)
    earlier = jnp.dot(hot.astype(BF), tri, preferred_element_type=F32)
    pos = jnp.sum(earlier * hot, axis=0, keepdims=True)
    target = idv * CAP + pos.astype(jnp.int32)
    chunk = 128

    def select_tokens(i, c):
        r0 = pl.multiple_of(i * chunk, chunk)
        m = ones_where(iota((chunk, pairs), 0) + r0 == target)
        both = sum(m[:, k * tokens : (k + 1) * tokens] for k in range(pairs // tokens))
        self_f[pl.ds(r0, chunk), :] = both.astype(BF)
        return c

    lax.fori_loop(0, ROWS // chunk, select_tokens, 0)

    def select_pairs():
        routes = pairs // tokens
        row = iota((pairs, pairs), 0)
        swap = ones_where((row % tokens) * routes + row // tokens == iota((pairs, pairs), 1))
        which = iota((8, pairs), 0) == 0
        both = jnp.where(which, idv.astype(F32), pos).astype(BF)
        both = jnp.dot(both, swap.astype(BF), preferred_element_type=F32)
        at = (both[0:1] * CAP + both[1:2]).astype(jnp.int32)

        def one(i, c):
            r0 = pl.multiple_of(i * chunk, chunk)
            sel[pl.ds(r0, chunk), :] = ones_where(iota((chunk, pairs), 0) + r0 == at).astype(BF)
            return c

        lax.fori_loop(0, ROWS // chunk, one, 0)

    def gather_columns(pan, ref, b):
        count = NG if pan["kind"] == "g" else NF
        at = [((b + i) * count + pan["J"]) * SUB for i in (0, 1)]
        return [ref[:, pl.ds(a, SUB)] for a in at]

    def arrange(p):
        pan = PANELS[p]
        j = pan["J"]
        if pan["kind"] == "g" and j == 0:
            select_pairs()
        for m in range(N_DP // 2):
            lanes = slice(2 * SUB * m, 2 * SUB * (m + 1))
            if pan["kind"] == "f":
                feat[j, :, lanes] = jnp.concatenate(gather_columns(pan, feats, 2 * m), axis=1)
            else:
                v = jnp.concatenate(gather_columns(pan, grads, 2 * m), axis=1)
                grad[j, :, lanes] = (v.astype(F32) * gates[...]).astype(BF)

    def build(p):
        pan = PANELS[p]
        arrange(p)
        src = feat.at[pan["J"]] if pan["kind"] == "f" else grad.at[pan["J"]]
        pick = self_f if pan["kind"] == "f" else sel

        def one(i, c):
            r0 = pl.multiple_of(i * 256, 256)
            v = jnp.dot(pick[pl.ds(r0, 256), :], src[...], preferred_element_type=F32)
            sb[pl.ds(pl.multiple_of(p * ROWS + r0, 256), 256), :] = v.astype(BF)
            return c

        lax.fori_loop(0, ROWS // 256, one, 0)
        own = pl.multiple_of(p * ROWS + me * CAP, CAP)
        rb[pl.ds(own, CAP), :] = sb[pl.ds(own, CAP), :]

    def push(p):
        def one(r, c):
            q, dev = plane_peer(r)
            pltpu.make_async_remote_copy(
                src_ref=sb.at[pl.ds(pl.multiple_of(p * ROWS + q * CAP, CAP), CAP), :],
                dst_ref=rb.at[pl.ds(pl.multiple_of(p * ROWS + me * CAP, CAP), CAP), :],
                send_sem=a_send.at[p],
                recv_sem=a_recv.at[p],
                device_id=dev,
                device_id_type=MESH,
            ).start()
            return c

        lax.fori_loop(1, E, one, 0)

    def wait_rows(ref, rows, sem):
        v = ref.at[pl.ds(0, rows), :]
        pltpu.make_async_copy(v, v, sem).wait()

    def compute(p):
        pan = PANELS[p]
        f0 = pan["first"]

        def one(i, c):
            k = i // 2
            h = i % 2
            a = rb[pl.ds(p * ROWS, ROWS), pl.ds(pl.multiple_of(h * 256, 256), 256)]
            b = rb[pl.ds(pl.multiple_of((f0 + k) * ROWS, ROWS), ROWS), :]
            v = lax.dot_general(a, b, (((0,), (0,)), ((), ())), preferred_element_type=F32)
            gram[pl.ds(pl.multiple_of((pan["ub"] + k) * W + h * 256, 256), 256), :] = v
            return c

        lax.fori_loop(0, 2 * (pan["J"] + 1), one, 0)

    def piece(pan, k, s, b):
        r = (pan["ub"] + k) * W + b * SUB + (s % 2) * PR
        lanes = pl.ds(pl.multiple_of((s // 2) * PC, PC), PC)
        return gram[pl.ds(pl.multiple_of(r, PR), PR), lanes]

    def seg(pan, t, h, k=0, i=0):
        return (t * PIECES + pan["rb"] + h * half_pieces(pan["J"]) + k * HALF + i) * PR

    def height(pan):
        return half_pieces(pan["J"]) * PR

    def remote(src, dst, ss, rs, dev):
        return pltpu.make_async_remote_copy(
            src_ref=src, dst_ref=dst, send_sem=ss, recv_sem=rs, device_id=dev, device_id_type=MESH
        )

    def ring(p, t, way, h):
        pan = PANELS[p]
        buf, ss, rs, dev = (
            (rsd, d_send, d_recv, down) if way == "d" else (rsu, u_send, u_recv, up)
        )
        n = height(pan)
        if t == 1:
            src = st.at[pl.ds(seg(pan, 0, h), n), :]
        else:
            src = buf.at[pl.ds(seg(pan, t - 2, h), n), :]
        dst = buf.at[pl.ds(seg(pan, t - 1, h), n), :]
        i = (p * 4 + t - 1) * 2 + h
        return remote(src, dst, ss.at[i], rs.at[i], dev)

    def over(pan, h, s, fn):
        def one(k, c):
            for i in range(HALF):
                fn(k, i, h * HALF + i)
            return c

        lax.fori_loop(0, pan["J"], one, 0)
        for i in range(DIAG):
            fn(pan["J"], i, (s // 2 * 2 + h * DIAG + i) % N_DP)

    def far(h):
        return "d" if h == 0 else "u"

    def ring_rows(pan, t, h, k, i):
        return pl.ds(pl.multiple_of(seg(pan, t, h, k, i), PR), PR)

    def step1(p):
        pan = PANELS[p]
        s = (z + 4) % N_Z
        for h in (0, 1):

            def one(k, i, b):
                st[ring_rows(pan, 0, h, k, i), :] = piece(pan, k, s, b).astype(BF)

            over(pan, h, s, one)
            ring(p, 1, far(h), h).start()

    def step(p, t, h):
        pan = PANELS[p]
        order = ("d", "u") if far(h) == "u" else ("u", "d")
        for way in order:
            buf = rsd if way == "d" else rsu
            dist = 5 - t
            s = (z + N_Z - dist) % N_Z if way == "d" else (z + dist) % N_Z
            fresh = t == 2 and way != far(h)
            if not fresh:
                ring(p, t - 1, way, h).wait_recv()

            def one(k, i, b):
                r = ring_rows(pan, t - 2, h, k, i)
                own = piece(pan, k, s, b)
                if not fresh:
                    own = own + buf[r, :].astype(F32)
                buf[r, :] = own.astype(BF)

            over(pan, h, s, one)
            ring(p, t, way, h).start()

    def slot(pan, q, k=0):
        return pan["ub"] * N_DP + q * (pan["J"] + 1) + k

    def slots(pan, q):
        return pl.ds(slot(pan, q), pan["J"] + 1)

    def place(pan, q):
        return (
            pl.ds(pan["ub"], pan["J"] + 1),
            pl.ds(pl.multiple_of((q % 2) * PR, PR), PR),
            pl.ds(pl.multiple_of((q // 2) * PC, PC), PC),
        )

    def finish(p):
        pan = PANELS[p]
        for h in (0, 1):
            ring(p, 4, "d", h).wait_recv()
            ring(p, 4, "u", h).wait_recv()

            def one(k, i, b):
                r = ring_rows(pan, 3, h, k, i)
                v = piece(pan, k, z, b) + rsd[r, :].astype(F32) + rsu[r, :].astype(F32)
                ts[slot(pan, b, k)] = v.astype(BF)

            over(pan, h, z, one)
        for i in range(2 * DIAG, N_DP):
            ts[slot(pan, (z // 2 * 2 + i) % N_DP, pan["J"])] = jnp.zeros((PR, PC), BF)

        def one_peer(r, c):
            b = (dp + r) % N_DP
            remote(
                ts.at[slots(pan, b)], tx.at[slots(pan, dp)], x_send.at[p], x_recv.at[p], (b, ex)
            ).start()
            return c

        lax.fori_loop(1, N_DP, one_peer, 0)
        tx[slots(pan, dp)] = ts[slots(pan, dp)]

    def turn(p):
        pan = PANELS[p]
        wait_slots(pan, x_recv.at[p])

        def one_peer(r, c):
            q, dev = line_peer(r)
            remote(
                tx.at[slots(pan, q)], tr.at[place(pan, z)], z_send.at[p], z_recv.at[p], dev
            ).start()
            return c

        lax.fori_loop(1, N_Z, one_peer, 0)
        tr[place(pan, z)] = tx[slots(pan, z)]

    def wait_slots(pan, sem):
        v = ts.at[pl.ds(0, (N_DP - 1) * (pan["J"] + 1))]
        pltpu.make_async_copy(v, v, sem).wait()

    def put(pan, row, col, v):
        out, count = (of, NF) if pan["kind"] == "f" else (og, NG)
        v = v.astype(BF)
        for b in range(N_DP):
            c = (b * count + col) * SUB
            out[0, pl.ds(row * SUB, SUB), pl.ds(c, SUB)] = v[:, b * SUB : (b + 1) * SUB]

    def tile_slot(pan, b):
        return pan["tb"] * N_DP + b * pan["J"]

    def wait_tiles(j, sem):
        v = tt.at[pl.ds(0, (N_DP - 1) * j)]
        pltpu.make_async_copy(v, v, sem).wait()

    def spread(p):
        pan = PANELS[p]
        j = pan["J"]
        wait_slots(pan, z_recv.at[p])
        if j > 0:
            mine = pl.ds(pan["ub"], j)
            dst = pl.ds(tile_slot(pan, dp), j)

            def one(r, c):
                b = (dp + r) % N_DP
                lanes = pl.ds(pl.multiple_of((b // 2) * 128, 128), 128)
                remote(
                    tr.at[mine, :, lanes], tt.at[dst], m_send.at[p], m_recv.at[p], (b, ex)
                ).start()
                return c

            lax.fori_loop(1, N_DP, one, 0)
            own_lanes = pl.ds(pl.multiple_of((dp // 2) * 128, 128), 128)
            tt[dst] = tr[mine, :, own_lanes]
        for i in (0, 1):
            e_copy(p, i).start()
        for k in range(j):
            put(pan, j, k, tr[pan["ub"] + k])

    def e_copy(p, i):
        pan = PANELS[p]
        m = (dp // 2 + N_DP // 2 - 1) % (N_DP // 2)
        lanes = pl.ds(pl.multiple_of(m * 128, 128), 128)
        return remote(
            tr.at[pan["ub"] + pan["J"], :, lanes],
            td.at[p * 2 + dp % 2],
            e_send.at[p],
            e_recv.at[p],
            (m * 2 + i, ex),
        )

    def wait_diag(sem):
        v = td.at[pl.ds(0, 2)]
        pltpu.make_async_copy(v, v, sem).wait()

    def collect(p):
        pan = PANELS[p]
        j = pan["J"]
        off = (dp % 2) * SUB
        pick = lax.broadcasted_iota(jnp.int32, (SUB, 128), 1) == (
            lax.broadcasted_iota(jnp.int32, (SUB, 128), 0) + off
        )
        pick = jnp.where(pick, 1.0, 0.0).astype(BF)
        wait_diag(e_recv.at[p])
        tiles = jnp.concatenate([td[p * 2], td[p * 2 + 1]], axis=0)
        v = lax.dot_general(pick, tiles, (((1,), (1,)), ((), ())), preferred_element_type=F32)
        parts = []
        for m in range(N_DP // 2):
            have = tr[pan["ub"] + j, :, m * 128 : (m + 1) * 128].astype(F32)
            parts.append(jnp.where((dp // 2 + 1) % (N_DP // 2) == m, v, have))
        put(pan, j, j, jnp.concatenate(parts, axis=1))
        if j > 0:
            wait_tiles(j, m_recv.at[p])
        for k in range(j):
            parts = [tt[tile_slot(pan, b) + k] for b in range(N_DP)]
            tiles = jnp.concatenate(parts, axis=0)
            v = lax.dot_general(pick, tiles, (((1,), (1,)), ((), ())), preferred_element_type=F32)
            put(pan, k, j, v)

    def land(p):
        wait_rows(rb, (E - 1) * CAP, a_recv.at[p])

    build(0)
    pl.semaphore_wait(barrier, E - 1 + N_Z - 1)
    push(0)
    for p in range(1, AHEAD):
        build(p)
        push(p)

    def front(p):
        land(p)
        if p + AHEAD < NP:
            build(p + AHEAD)
            push(p + AHEAD)
        compute(p)
        step1(p)

    for kind, p, h in make_order():
        if kind == "land":
            front(p)
        elif kind == "sum":
            finish(p)
        elif kind == "turn":
            turn(p)
        elif kind == "out":
            spread(p)
        elif kind == "tile":
            collect(p)
        else:
            step(p, kind, h)

    for p in range(NP):
        wait_rows(sb, (E - 1) * CAP, a_send.at[p])
        for h in (0, 1):
            ring(p, 1, far(h), h).wait_send()
            for t in (2, 3, 4):
                ring(p, t, "d", h).wait_send()
                ring(p, t, "u", h).wait_send()
        wait_slots(PANELS[p], x_send.at[p])
        wait_slots(PANELS[p], z_send.at[p])
        j = PANELS[p]["J"]
        wait_diag(e_send.at[p])
        if j > 0:
            wait_tiles(j, m_send.at[p])


def per_device(features, expert_ids, gate_weights, out_grads):
    tokens, width = features.shape
    routes, hidden = out_grads.shape[1:]
    pairs = routes * tokens
    nf, ng = width // W, hidden // W
    vm = pl.BlockSpec(memory_space=pltpu.VMEM)
    dma = pltpu.SemaphoreType.DMA
    of, og = pl.pallas_call(
        kernel,
        out_shape=(
            jax.ShapeDtypeStruct((1, nf * SUB, width), BF),
            jax.ShapeDtypeStruct((1, ng * SUB, hidden), BF),
        ),
        in_specs=[vm] * 4,
        out_specs=(vm, vm),
        scratch_shapes=[
            pltpu.VMEM((nf, tokens, W), BF),
            pltpu.VMEM((ng, pairs, W), BF),
            pltpu.VMEM((ROWS, pairs), BF),
            pltpu.VMEM((ROWS, tokens), BF),
            pltpu.VMEM((NP * ROWS, W), BF),
            pltpu.VMEM((NP * ROWS, W), BF),
            pltpu.VMEM((UNITS * W, W), F32),
            pltpu.VMEM((4 * PIECES * PR, PC), BF),
            pltpu.VMEM((4 * PIECES * PR, PC), BF),
            pltpu.VMEM((PIECES * PR, PC), BF),
            pltpu.VMEM((UNITS * N_DP, PR, PC), BF),
            pltpu.VMEM((UNITS * N_DP, PR, PC), BF),
            pltpu.VMEM((UNITS, SUB, W), BF),
            pltpu.VMEM((TUNITS * N_DP, SUB, 128), BF),
            pltpu.VMEM((NP * 2, SUB, 128), BF),
            dma((NP,)),
            dma((NP,)),
            dma((NP * 8,)),
            dma((NP * 8,)),
            dma((NP * 8,)),
            dma((NP * 8,)),
            dma((NP,)),
            dma((NP,)),
            dma((NP,)),
            dma((NP,)),
            dma((NP,)),
            dma((NP,)),
            dma((NP,)),
            dma((NP,)),
        ],
        compiler_params=pltpu.CompilerParams(
            collective_id=0, has_side_effects=True, vmem_limit_bytes=60 * 1024 * 1024
        ),
        cost_estimate=pl.CostEstimate(
            flops=9_000_000_000, bytes_accessed=8_000_000, transcendentals=0
        ),
    )(features, out_grads.reshape(pairs, hidden), gate_weights.reshape(pairs, 1), expert_ids.T)
    return of.astype(F32) * SCALE, og.astype(F32) * SCALE


def solution(mesh):
    in_specs = (
        P(("dp", "expert"), None),
        P(("dp", "expert"), None),
        P(("dp", "expert"), None),
        P(("dp", "expert"), None, None),
    )
    out_specs = (P("expert", "dp", None), P("expert", "dp", None))
    return jax.shard_map(
        per_device, mesh=mesh, in_specs=in_specs, out_specs=out_specs, check_vma=False
    )
```

```python
import jax
import jax.numpy as jnp
from jax import lax
from jax.experimental import pallas as pl
from jax.experimental.pallas import tpu as pltpu
from jax.sharding import PartitionSpec as P

MESH = pl.DeviceIdType.MESH
BF = jnp.bfloat16
F32 = jnp.float32

N_DP = 8
N_Z = 8
N_Y = 4
E = 32
CAP = 32
ROWS = E * CAP
W = 512
SUB = 64
SCALE = 1.0 / 1024.0


PR, PC = 32, 128
HALF = N_DP // 2
DIAG = 3


def half_pieces(j):
    return j * HALF + DIAG


def make_panels(nf, ng):
    panels = []
    ub = tb = rb = 0
    for kind, count in (("f", nf), ("g", ng)):
        for j in range(count):
            panels.append(dict(kind=kind, J=j, ub=ub, tb=tb, rb=rb, first=len(panels) - j))
            ub += j + 1
            tb += j
            rb += 2 * half_pieces(j)
    return panels, ub, tb, rb


NF, NG = 4, 3
PANELS, UNITS, TUNITS, PIECES = make_panels(NF, NG)
NP = len(PANELS)
AHEAD = 2


def make_order(first=8.0, every=12.5, hop=1.6, lag=2.5, move_lag=4.0, x_lag=15.0):
    ready = {("land", p, 0): first + every * (p + 1) for p in range(NP)}
    link = now = 0.0
    order = []
    halves = dict.fromkeys(range(NP), 0)
    while ready:
        now = max(now, min(ready.values()))
        op = min(ready, key=lambda o: (ready[o], o[1], str(o[0]), o[2]))
        del ready[op]
        order.append(op)
        kind, p, h = op
        size = PANELS[p]["J"] + 1
        ring_size = PANELS[p]["J"] + 0.75
        if kind == "land":
            now += 1.3 * size + 3.0
            for h in (0, 1):
                link = max(link, now) + 0.25 * hop * ring_size
                ready[(2, p, h)] = link + lag
        elif kind == "sum":
            now += 0.3 * size + 0.3
            ready[("turn", p, 0)] = now + 0.5 * size + x_lag
        elif kind == "turn":
            now += 0.3
            link = max(link, now) + hop * size
            ready[("out", p, 0)] = link + move_lag
        elif kind == "out":
            now += 0.3 * size + 0.3
            ready[("tile", p, 0)] = now + x_lag + size
        elif kind == "tile":
            now += 0.5 * size
        else:
            now += 0.2 * size + 0.15
            link = max(link, now) + 0.5 * hop * ring_size
            if kind < 4:
                ready[(kind + 1, p, h)] = link + lag
            else:
                halves[p] += 1
                if halves[p] == 2:
                    ready[("sum", p, 0)] = link + lag
    return order


def kernel(
    feats, raw, gates, ids, of, og,
    grads, scaled, panel_f, panel_g, sel, self_f, sb, rb, gram, rsd, rsu, st, ts, tx, tr, tt, td,
    a_send, a_recv, d_send, d_recv, u_send, u_recv,
    raw_sem, x_send, x_recv, z_send, z_recv, m_send, m_recv, e_send, e_recv,
):
    dp = lax.axis_index("dp")
    ex = lax.axis_index("expert")
    z = ex // N_Y
    y = ex % N_Y
    me = dp * N_Y + y

    def plane_peer(r):
        q = (me + r) % E
        return q, (q // N_Y, z * N_Y + q % N_Y)

    def line_peer(r):
        q = (z + r) % N_Z
        return q, (dp, q * N_Y + y)

    down = (dp, ((z + N_Z - 1) % N_Z) * N_Y + y)
    up = (dp, ((z + 1) % N_Z) * N_Y + y)

    raw_copy = pltpu.make_async_copy(raw, grads, raw_sem)
    raw_copy.start()
    barrier = pltpu.get_barrier_semaphore()

    def greet(r, c):
        pl.semaphore_signal(barrier, inc=1, device_id=plane_peer(r)[1], device_id_type=MESH)
        return c

    def greet_line(r, c):
        pl.semaphore_signal(barrier, inc=1, device_id=line_peer(r)[1], device_id_type=MESH)
        return c

    lax.fori_loop(1, E, greet, 0)
    lax.fori_loop(1, N_Z, greet_line, 0)

    tokens = feats.shape[0]
    routes = gates.shape[0]
    pairs = routes * tokens
    idv = jnp.concatenate([ids[k : k + 1, :] for k in range(routes)], axis=1)

    def iota(shape, dim):
        return lax.broadcasted_iota(jnp.int32, shape, dim)

    def ones_where(m):
        return jnp.where(m, 1.0, 0.0)

    hot = ones_where(iota((E, pairs), 0) == idv)
    tri = ones_where(iota((pairs, pairs), 0) < iota((pairs, pairs), 1)).astype(BF)
    earlier = jnp.dot(hot.astype(BF), tri, preferred_element_type=F32)
    pos = jnp.sum(earlier * hot, axis=0, keepdims=True)
    target = idv * CAP + pos.astype(jnp.int32)
    chunk = 128

    def select_tokens(i, c):
        r0 = pl.multiple_of(i * chunk, chunk)
        m = ones_where(iota((chunk, pairs), 0) + r0 == target)
        both = sum(m[:, k * tokens : (k + 1) * tokens] for k in range(routes))
        self_f[pl.ds(r0, chunk), :] = both.astype(BF)
        return c

    lax.fori_loop(0, ROWS // chunk, select_tokens, 0)

    def select_pairs(i, c):
        r0 = pl.multiple_of(i * chunk, chunk)
        sel[pl.ds(r0, chunk), :] = ones_where(iota((chunk, pairs), 0) + r0 == target).astype(BF)
        return c

    def scale_grads():
        raw_copy.wait()
        weights = [jnp.broadcast_to(gates[k : k + 1, :], (128, tokens)).T for k in range(routes)]
        for i in range(grads.shape[2] // 128):
            lanes = slice(i * 128, (i + 1) * 128)
            for k in range(routes):
                v = grads[:, k, lanes].astype(F32) * weights[k]
                scaled[k * tokens : (k + 1) * tokens, lanes] = v.astype(BF)

    def gather_columns(pan, ref, b):
        count = NG if pan["kind"] == "g" else NF
        at = [((b + i) * count + pan["J"]) * SUB for i in (0, 1)]
        return [ref[:, pl.ds(a, SUB)] for a in at]

    def arrange(p):
        pan = PANELS[p]
        src, dst = (feats, panel_f) if pan["kind"] == "f" else (scaled, panel_g)
        for m in range(N_DP // 2):
            lanes = slice(2 * SUB * m, 2 * SUB * (m + 1))
            dst[:, lanes] = jnp.concatenate(gather_columns(pan, src, 2 * m), axis=1)

    def build(p):
        pan = PANELS[p]
        arrange(p)
        src = panel_f if pan["kind"] == "f" else panel_g
        pick = self_f if pan["kind"] == "f" else sel

        def one(i, c):
            r0 = pl.multiple_of(i * 256, 256)
            v = jnp.dot(pick[pl.ds(r0, 256), :], src[...], preferred_element_type=F32)
            sb[pl.ds(pl.multiple_of(p * ROWS + r0, 256), 256), :] = v.astype(BF)
            return c

        lax.fori_loop(0, ROWS // 256, one, 0)
        own = pl.multiple_of(p * ROWS + me * CAP, CAP)
        rb[pl.ds(own, CAP), :] = sb[pl.ds(own, CAP), :]

    def push(p):
        def one(r, c):
            q, dev = plane_peer(r)
            pltpu.make_async_remote_copy(
                src_ref=sb.at[pl.ds(pl.multiple_of(p * ROWS + q * CAP, CAP), CAP), :],
                dst_ref=rb.at[pl.ds(pl.multiple_of(p * ROWS + me * CAP, CAP), CAP), :],
                send_sem=a_send.at[p],
                recv_sem=a_recv.at[p],
                device_id=dev,
                device_id_type=MESH,
            ).start()
            return c

        lax.fori_loop(1, E, one, 0)

    def wait_rows(ref, rows, sem):
        v = ref.at[pl.ds(0, rows), :]
        pltpu.make_async_copy(v, v, sem).wait()

    def compute(p):
        pan = PANELS[p]
        f0 = pan["first"]

        def one(i, c):
            k = i // 2
            h = i % 2
            a = rb[pl.ds(p * ROWS, ROWS), pl.ds(pl.multiple_of(h * 256, 256), 256)]
            b = rb[pl.ds(pl.multiple_of((f0 + k) * ROWS, ROWS), ROWS), :]
            v = lax.dot_general(a, b, (((0,), (0,)), ((), ())), preferred_element_type=F32)
            gram[pl.ds(pl.multiple_of((pan["ub"] + k) * W + h * 256, 256), 256), :] = v
            return c

        lax.fori_loop(0, 2 * (pan["J"] + 1), one, 0)

    def piece(pan, k, s, b):
        r = (pan["ub"] + k) * W + b * SUB + (s % 2) * PR
        lanes = pl.ds(pl.multiple_of((s // 2) * PC, PC), PC)
        return gram[pl.ds(pl.multiple_of(r, PR), PR), lanes]

    def seg(pan, t, h, k=0, i=0):
        return (t * PIECES + pan["rb"] + h * half_pieces(pan["J"]) + k * HALF + i) * PR

    def height(pan):
        return half_pieces(pan["J"]) * PR

    def remote(src, dst, ss, rs, dev):
        return pltpu.make_async_remote_copy(
            src_ref=src, dst_ref=dst, send_sem=ss, recv_sem=rs, device_id=dev, device_id_type=MESH
        )

    def ring(p, t, way, h):
        pan = PANELS[p]
        buf, ss, rs, dev = (
            (rsd, d_send, d_recv, down) if way == "d" else (rsu, u_send, u_recv, up)
        )
        n = height(pan)
        if t == 1:
            src = st.at[pl.ds(seg(pan, 0, h), n), :]
        else:
            src = buf.at[pl.ds(seg(pan, t - 2, h), n), :]
        dst = buf.at[pl.ds(seg(pan, t - 1, h), n), :]
        i = (p * 4 + t - 1) * 2 + h
        return remote(src, dst, ss.at[i], rs.at[i], dev)

    def over(pan, h, s, fn):
        def one(k, c):
            for i in range(HALF):
                fn(k, i, h * HALF + i)
            return c

        lax.fori_loop(0, pan["J"], one, 0)
        for i in range(DIAG):
            fn(pan["J"], i, (s // 2 * 2 + h * DIAG + i) % N_DP)

    def far(h):
        return "d" if h == 0 else "u"

    def ring_rows(pan, t, h, k, i):
        return pl.ds(pl.multiple_of(seg(pan, t, h, k, i), PR), PR)

    def step1(p):
        pan = PANELS[p]
        s = (z + 4) % N_Z
        for h in (0, 1):

            def one(k, i, b):
                st[ring_rows(pan, 0, h, k, i), :] = piece(pan, k, s, b).astype(BF)

            over(pan, h, s, one)
            ring(p, 1, far(h), h).start()

    def step(p, t, h):
        pan = PANELS[p]
        order = ("d", "u") if far(h) == "u" else ("u", "d")
        for way in order:
            buf = rsd if way == "d" else rsu
            dist = 5 - t
            s = (z + N_Z - dist) % N_Z if way == "d" else (z + dist) % N_Z
            fresh = t == 2 and way != far(h)
            if not fresh:
                ring(p, t - 1, way, h).wait_recv()

            def one(k, i, b):
                r = ring_rows(pan, t - 2, h, k, i)
                own = piece(pan, k, s, b)
                if not fresh:
                    own = own + buf[r, :].astype(F32)
                buf[r, :] = own.astype(BF)

            over(pan, h, s, one)
            ring(p, t, way, h).start()

    def slot(pan, q, k=0):
        return pan["ub"] * N_DP + q * (pan["J"] + 1) + k

    def slots(pan, q):
        return pl.ds(slot(pan, q), pan["J"] + 1)

    def place(pan, q):
        return (
            pl.ds(pan["ub"], pan["J"] + 1),
            pl.ds(pl.multiple_of((q % 2) * PR, PR), PR),
            pl.ds(pl.multiple_of((q // 2) * PC, PC), PC),
        )

    def finish(p):
        pan = PANELS[p]
        for h in (0, 1):
            ring(p, 4, "d", h).wait_recv()
            ring(p, 4, "u", h).wait_recv()

            def one(k, i, b):
                r = ring_rows(pan, 3, h, k, i)
                v = piece(pan, k, z, b) + rsd[r, :].astype(F32) + rsu[r, :].astype(F32)
                ts[slot(pan, b, k)] = v.astype(BF)

            over(pan, h, z, one)
        for i in range(2 * DIAG, N_DP):
            ts[slot(pan, (z // 2 * 2 + i) % N_DP, pan["J"])] = jnp.zeros((PR, PC), BF)

        def one_peer(r, c):
            b = (dp + r) % N_DP
            remote(
                ts.at[slots(pan, b)], tx.at[slots(pan, dp)], x_send.at[p], x_recv.at[p], (b, ex)
            ).start()
            return c

        lax.fori_loop(1, N_DP, one_peer, 0)
        tx[slots(pan, dp)] = ts[slots(pan, dp)]

    def turn(p):
        pan = PANELS[p]
        wait_slots(pan, x_recv.at[p])

        def one_peer(r, c):
            q, dev = line_peer(r)
            remote(
                tx.at[slots(pan, q)], tr.at[place(pan, z)], z_send.at[p], z_recv.at[p], dev
            ).start()
            return c

        lax.fori_loop(1, N_Z, one_peer, 0)
        tr[place(pan, z)] = tx[slots(pan, z)]

    def wait_slots(pan, sem):
        v = ts.at[pl.ds(0, (N_DP - 1) * (pan["J"] + 1))]
        pltpu.make_async_copy(v, v, sem).wait()

    def put(pan, row, col, v):
        out, count = (of, NF) if pan["kind"] == "f" else (og, NG)
        v = v.astype(BF)
        for b in range(N_DP):
            c = (b * count + col) * SUB
            out[0, pl.ds(row * SUB, SUB), pl.ds(c, SUB)] = v[:, b * SUB : (b + 1) * SUB]

    def tile_slot(pan, b):
        return pan["tb"] * N_DP + b * pan["J"]

    def wait_tiles(j, sem):
        v = tt.at[pl.ds(0, (N_DP - 1) * j)]
        pltpu.make_async_copy(v, v, sem).wait()

    def spread(p):
        pan = PANELS[p]
        j = pan["J"]
        wait_slots(pan, z_recv.at[p])
        if j > 0:
            mine = pl.ds(pan["ub"], j)
            dst = pl.ds(tile_slot(pan, dp), j)

            def one(r, c):
                b = (dp + r) % N_DP
                lanes = pl.ds(pl.multiple_of((b // 2) * 128, 128), 128)
                remote(
                    tr.at[mine, :, lanes], tt.at[dst], m_send.at[p], m_recv.at[p], (b, ex)
                ).start()
                return c

            lax.fori_loop(1, N_DP, one, 0)
            own_lanes = pl.ds(pl.multiple_of((dp // 2) * 128, 128), 128)
            tt[dst] = tr[mine, :, own_lanes]
        for i in (0, 1):
            e_copy(p, i).start()
        for k in range(j):
            put(pan, j, k, tr[pan["ub"] + k])

    def e_copy(p, i):
        pan = PANELS[p]
        m = (dp // 2 + N_DP // 2 - 1) % (N_DP // 2)
        lanes = pl.ds(pl.multiple_of(m * 128, 128), 128)
        return remote(
            tr.at[pan["ub"] + pan["J"], :, lanes],
            td.at[p * 2 + dp % 2],
            e_send.at[p],
            e_recv.at[p],
            (m * 2 + i, ex),
        )

    def wait_diag(sem):
        v = td.at[pl.ds(0, 2)]
        pltpu.make_async_copy(v, v, sem).wait()

    def collect(p):
        pan = PANELS[p]
        j = pan["J"]
        off = (dp % 2) * SUB
        pick = lax.broadcasted_iota(jnp.int32, (SUB, 128), 1) == (
            lax.broadcasted_iota(jnp.int32, (SUB, 128), 0) + off
        )
        pick = jnp.where(pick, 1.0, 0.0).astype(BF)
        wait_diag(e_recv.at[p])
        tiles = jnp.concatenate([td[p * 2], td[p * 2 + 1]], axis=0)
        v = lax.dot_general(pick, tiles, (((1,), (1,)), ((), ())), preferred_element_type=F32)
        parts = []
        for m in range(N_DP // 2):
            have = tr[pan["ub"] + j, :, m * 128 : (m + 1) * 128].astype(F32)
            parts.append(jnp.where((dp // 2 + 1) % (N_DP // 2) == m, v, have))
        put(pan, j, j, jnp.concatenate(parts, axis=1))
        if j > 0:
            wait_tiles(j, m_recv.at[p])
        for k in range(j):
            parts = [tt[tile_slot(pan, b) + k] for b in range(N_DP)]
            tiles = jnp.concatenate(parts, axis=0)
            v = lax.dot_general(pick, tiles, (((1,), (1,)), ((), ())), preferred_element_type=F32)
            put(pan, k, j, v)

    def land(p):
        wait_rows(rb, (E - 1) * CAP, a_recv.at[p])

    build(0)
    pl.semaphore_wait(barrier, E - 1 + N_Z - 1)
    push(0)
    for p in range(1, AHEAD):
        build(p)
        push(p)
    lax.fori_loop(0, ROWS // chunk, select_pairs, 0)
    scale_grads()

    def front(p):
        land(p)
        if p + AHEAD < NP:
            build(p + AHEAD)
            push(p + AHEAD)
        compute(p)
        step1(p)

    for kind, p, h in make_order():
        if kind == "land":
            front(p)
        elif kind == "sum":
            finish(p)
        elif kind == "turn":
            turn(p)
        elif kind == "out":
            spread(p)
        elif kind == "tile":
            collect(p)
        else:
            step(p, kind, h)

    for p in range(NP):
        wait_rows(sb, (E - 1) * CAP, a_send.at[p])
        for h in (0, 1):
            ring(p, 1, far(h), h).wait_send()
            for t in (2, 3, 4):
                ring(p, t, "d", h).wait_send()
                ring(p, t, "u", h).wait_send()
        wait_slots(PANELS[p], x_send.at[p])
        wait_slots(PANELS[p], z_send.at[p])
        j = PANELS[p]["J"]
        wait_diag(e_send.at[p])
        if j > 0:
            wait_tiles(j, m_send.at[p])


def finalize(f_in, g_in, f_out, g_out):
    f_out[...] = f_in[...].astype(F32) * SCALE
    g_out[...] = g_in[...].astype(F32) * SCALE


def per_device(features, expert_ids, gate_weights, out_grads):
    tokens, width = features.shape
    routes, hidden = out_grads.shape[1:]
    pairs = routes * tokens
    nf, ng = width // W, hidden // W
    vm = pl.BlockSpec(memory_space=pltpu.VMEM)
    hbm = pl.BlockSpec(memory_space=pl.ANY)
    dma = pltpu.SemaphoreType.DMA
    of, og = pl.pallas_call(
        kernel,
        out_shape=(
            jax.ShapeDtypeStruct((1, nf * SUB, width), BF),
            jax.ShapeDtypeStruct((1, ng * SUB, hidden), BF),
        ),
        in_specs=[vm, hbm, vm, vm],
        out_specs=(vm, vm),
        scratch_shapes=[
            pltpu.VMEM((tokens, routes, hidden), BF),
            pltpu.VMEM((pairs, hidden), BF),
            pltpu.VMEM((tokens, W), BF),
            pltpu.VMEM((pairs, W), BF),
            pltpu.VMEM((ROWS, pairs), BF),
            pltpu.VMEM((ROWS, tokens), BF),
            pltpu.VMEM((NP * ROWS, W), BF),
            pltpu.VMEM((NP * ROWS, W), BF),
            pltpu.VMEM((UNITS * W, W), F32),
            pltpu.VMEM((4 * PIECES * PR, PC), BF),
            pltpu.VMEM((4 * PIECES * PR, PC), BF),
            pltpu.VMEM((PIECES * PR, PC), BF),
            pltpu.VMEM((UNITS * N_DP, PR, PC), BF),
            pltpu.VMEM((UNITS * N_DP, PR, PC), BF),
            pltpu.VMEM((UNITS, SUB, W), BF),
            pltpu.VMEM((TUNITS * N_DP, SUB, 128), BF),
            pltpu.VMEM((NP * 2, SUB, 128), BF),
            dma((NP,)),
            dma((NP,)),
            dma((NP * 8,)),
            dma((NP * 8,)),
            dma((NP * 8,)),
            dma((NP * 8,)),
            dma,
            dma((NP,)),
            dma((NP,)),
            dma((NP,)),
            dma((NP,)),
            dma((NP,)),
            dma((NP,)),
            dma((NP,)),
            dma((NP,)),
        ],
        compiler_params=pltpu.CompilerParams(
            collective_id=0, has_side_effects=True, vmem_limit_bytes=60 * 1024 * 1024
        ),
        cost_estimate=pl.CostEstimate(
            flops=9_000_000_000, bytes_accessed=8_000_000, transcendentals=0
        ),
    )(features, out_grads, gate_weights.T, expert_ids.T)
    steps = 4

    def block(x):
        return pl.BlockSpec((1, x.shape[1] // steps, x.shape[2]), lambda i: (0, i, 0))

    return pl.pallas_call(
        finalize,
        grid=(steps,),
        out_shape=tuple(jax.ShapeDtypeStruct(x.shape, F32) for x in (of, og)),
        in_specs=[block(of), block(og)],
        out_specs=(block(of), block(og)),
    )(of, og)


def solution(mesh):
    in_specs = (
        P(("dp", "expert"), None),
        P(("dp", "expert"), None),
        P(("dp", "expert"), None),
        P(("dp", "expert"), None, None),
    )
    out_specs = (P("expert", "dp", None), P("expert", "dp", None))
    return jax.shard_map(
        per_device, mesh=mesh, in_specs=in_specs, out_specs=out_specs, check_vma=False
    )
```

```python
import jax
import jax.numpy as jnp
from jax import lax
from jax.experimental import pallas as pl
from jax.experimental.pallas import tpu as pltpu
from jax.sharding import PartitionSpec as P

MESH = pl.DeviceIdType.MESH
BF = jnp.bfloat16
F32 = jnp.float32

N_DP = 8
N_Z = 8
N_Y = 4
E = 32
CAP = 32
ROWS = E * CAP
W = 512
SUB = 64
SCALE = 1.0 / 1024.0


PR, PC = 32, 128
HALF = N_DP // 2
DIAG = 3


def half_pieces(j):
    return j * HALF + DIAG


def make_panels(nf, ng):
    panels = []
    ub = tb = rb = 0
    for kind, count in (("f", nf), ("g", ng)):
        for j in range(count):
            panels.append(dict(kind=kind, J=j, ub=ub, tb=tb, rb=rb, first=len(panels) - j))
            ub += j + 1
            tb += j
            rb += 2 * half_pieces(j)
    return panels, ub, tb, rb


NF, NG = 4, 3
PANELS, UNITS, TUNITS, PIECES = make_panels(NF, NG)
NP = len(PANELS)
AHEAD = 2


def make_order(first=8.0, every=15.0, hop=1.6, lag=2.5, move_lag=4.0, x_lag=15.0):
    ready = {("land", p, 0): first + every * (p + 1) for p in range(NP)}
    link = now = 0.0
    order = []
    halves = dict.fromkeys(range(NP), 0)
    while ready:
        now = max(now, min(ready.values()))
        op = min(ready, key=lambda o: (ready[o] - (4.0 if o[1] >= 5 else 0.0), o[1], str(o[0]), o[2]))
        del ready[op]
        order.append(op)
        kind, p, h = op
        size = PANELS[p]["J"] + 1
        ring_size = PANELS[p]["J"] + 0.75
        if kind == "land":
            now += 1.3 * size + 3.0
            for h in (0, 1):
                link = max(link, now) + 0.25 * hop * ring_size
                ready[(2, p, h)] = link + lag
        elif kind == "sum":
            now += 0.3 * size + 0.3
            ready[("turn", p, 0)] = now + 0.5 * size + x_lag
        elif kind == "turn":
            now += 0.3
            link = max(link, now) + hop * size
            ready[("out", p, 0)] = link + move_lag
        elif kind == "out":
            now += 0.3 * size + 0.3
            ready[("tile", p, 0)] = now + x_lag + size
        elif kind == "tile":
            now += 0.5 * size
        else:
            now += 0.2 * size + 0.15
            link = max(link, now) + 0.5 * hop * ring_size
            if kind < 4:
                ready[(kind + 1, p, h)] = link + lag
            else:
                halves[p] += 1
                if halves[p] == 2:
                    ready[("sum", p, 0)] = link + lag
    return order


def kernel(
    feats, raw, gates, ids, of, og,
    grads, scaled, panel_f, panel_g, sel, self_f, sb, rb, gram, rsd, rsu, st, ts, tx, tr, tt, td,
    a_send, a_recv, d_send, d_recv, u_send, u_recv,
    raw_sem, x_send, x_recv, z_send, z_recv, m_send, m_recv, e_send, e_recv,
):
    dp = lax.axis_index("dp")
    ex = lax.axis_index("expert")
    z = ex // N_Y
    y = ex % N_Y
    me = dp * N_Y + y

    def plane_peer(r):
        q = (me + r) % E
        return q, (q // N_Y, z * N_Y + q % N_Y)

    def line_peer(r):
        q = (z + r) % N_Z
        return q, (dp, q * N_Y + y)

    down = (dp, ((z + N_Z - 1) % N_Z) * N_Y + y)
    up = (dp, ((z + 1) % N_Z) * N_Y + y)

    raw_copy = pltpu.make_async_copy(raw, grads, raw_sem)
    raw_copy.start()
    barrier = pltpu.get_barrier_semaphore()

    def greet(r, c):
        pl.semaphore_signal(barrier, inc=1, device_id=plane_peer(r)[1], device_id_type=MESH)
        return c

    def greet_line(r, c):
        pl.semaphore_signal(barrier, inc=1, device_id=line_peer(r)[1], device_id_type=MESH)
        return c

    lax.fori_loop(1, E, greet, 0)
    lax.fori_loop(1, N_Z, greet_line, 0)

    tokens = feats.shape[0]
    routes = gates.shape[0]
    pairs = routes * tokens
    idv = jnp.concatenate([ids[k : k + 1, :] for k in range(routes)], axis=1)

    def iota(shape, dim):
        return lax.broadcasted_iota(jnp.int32, shape, dim)

    def ones_where(m):
        return jnp.where(m, 1.0, 0.0)

    hot = ones_where(iota((E, pairs), 0) == idv)
    tri = ones_where(iota((pairs, pairs), 0) < iota((pairs, pairs), 1)).astype(BF)
    earlier = jnp.dot(hot.astype(BF), tri, preferred_element_type=F32)
    pos = jnp.sum(earlier * hot, axis=0, keepdims=True)
    target = idv * CAP + pos.astype(jnp.int32)
    chunk = 128

    def select_tokens(i, c):
        r0 = pl.multiple_of(i * chunk, chunk)
        m = ones_where(iota((chunk, pairs), 0) + r0 == target)
        both = sum(m[:, k * tokens : (k + 1) * tokens] for k in range(routes))
        self_f[pl.ds(r0, chunk), :] = both.astype(BF)
        return c

    lax.fori_loop(0, ROWS // chunk, select_tokens, 0)

    def select_pairs(i, c):
        r0 = pl.multiple_of(i * chunk, chunk)
        sel[pl.ds(r0, chunk), :] = ones_where(iota((chunk, pairs), 0) + r0 == target).astype(BF)
        return c

    def scale_grads():
        raw_copy.wait()
        weights = [jnp.broadcast_to(gates[k : k + 1, :], (128, tokens)).T for k in range(routes)]
        for i in range(grads.shape[2] // 128):
            lanes = slice(i * 128, (i + 1) * 128)
            for k in range(routes):
                v = grads[:, k, lanes].astype(F32) * weights[k]
                scaled[k * tokens : (k + 1) * tokens, lanes] = v.astype(BF)

    def gather_columns(pan, ref, b):
        count = NG if pan["kind"] == "g" else NF
        at = [((b + i) * count + pan["J"]) * SUB for i in (0, 1)]
        return [ref[:, pl.ds(a, SUB)] for a in at]

    def arrange(p):
        pan = PANELS[p]
        src, dst = (feats, panel_f) if pan["kind"] == "f" else (scaled, panel_g)
        for m in range(N_DP // 2):
            lanes = slice(2 * SUB * m, 2 * SUB * (m + 1))
            dst[:, lanes] = jnp.concatenate(gather_columns(pan, src, 2 * m), axis=1)

    def build(p):
        pan = PANELS[p]
        arrange(p)
        src = panel_f if pan["kind"] == "f" else panel_g
        pick = self_f if pan["kind"] == "f" else sel

        def one(i, c):
            r0 = pl.multiple_of(i * 256, 256)
            v = jnp.dot(pick[pl.ds(r0, 256), :], src[...], preferred_element_type=F32)
            sb[pl.ds(pl.multiple_of(p * ROWS + r0, 256), 256), :] = v.astype(BF)
            return c

        lax.fori_loop(0, ROWS // 256, one, 0)
        own = pl.multiple_of(p * ROWS + me * CAP, CAP)
        rb[pl.ds(own, CAP), :] = sb[pl.ds(own, CAP), :]

    def push(p):
        def one(r, c):
            q, dev = plane_peer(r)
            pltpu.make_async_remote_copy(
                src_ref=sb.at[pl.ds(pl.multiple_of(p * ROWS + q * CAP, CAP), CAP), :],
                dst_ref=rb.at[pl.ds(pl.multiple_of(p * ROWS + me * CAP, CAP), CAP), :],
                send_sem=a_send.at[p],
                recv_sem=a_recv.at[p],
                device_id=dev,
                device_id_type=MESH,
            ).start()
            return c

        lax.fori_loop(1, E, one, 0)

    def wait_rows(ref, rows, sem):
        v = ref.at[pl.ds(0, rows), :]
        pltpu.make_async_copy(v, v, sem).wait()

    def compute(p):
        pan = PANELS[p]
        f0 = pan["first"]

        def one(i, c):
            k = i // 2
            h = i % 2
            a = rb[pl.ds(p * ROWS, ROWS), pl.ds(pl.multiple_of(h * 256, 256), 256)]
            b = rb[pl.ds(pl.multiple_of((f0 + k) * ROWS, ROWS), ROWS), :]
            v = lax.dot_general(a, b, (((0,), (0,)), ((), ())), preferred_element_type=F32)
            gram[pl.ds(pl.multiple_of((pan["ub"] + k) * W + h * 256, 256), 256), :] = v
            return c

        lax.fori_loop(0, 2 * (pan["J"] + 1), one, 0)

    def piece(pan, k, s, b):
        r = (pan["ub"] + k) * W + b * SUB + (s % 2) * PR
        lanes = pl.ds(pl.multiple_of((s // 2) * PC, PC), PC)
        return gram[pl.ds(pl.multiple_of(r, PR), PR), lanes]

    def seg(pan, t, h, k=0, i=0):
        return (t * PIECES + pan["rb"] + h * half_pieces(pan["J"]) + k * HALF + i) * PR

    def height(pan):
        return half_pieces(pan["J"]) * PR

    def remote(src, dst, ss, rs, dev):
        return pltpu.make_async_remote_copy(
            src_ref=src, dst_ref=dst, send_sem=ss, recv_sem=rs, device_id=dev, device_id_type=MESH
        )

    def ring(p, t, way, h):
        pan = PANELS[p]
        buf, ss, rs, dev = (
            (rsd, d_send, d_recv, down) if way == "d" else (rsu, u_send, u_recv, up)
        )
        n = height(pan)
        if t == 1:
            src = st.at[pl.ds(seg(pan, 0, h), n), :]
        else:
            src = buf.at[pl.ds(seg(pan, t - 2, h), n), :]
        dst = buf.at[pl.ds(seg(pan, t - 1, h), n), :]
        i = (p * 4 + t - 1) * 2 + h
        return remote(src, dst, ss.at[i], rs.at[i], dev)

    def over(pan, h, s, fn):
        def one(k, c):
            for i in range(HALF):
                fn(k, i, h * HALF + i)
            return c

        lax.fori_loop(0, pan["J"], one, 0)
        for i in range(DIAG):
            fn(pan["J"], i, (s // 2 * 2 + h * DIAG + i) % N_DP)

    def far(h):
        return "d" if h == 0 else "u"

    def ring_rows(pan, t, h, k, i):
        return pl.ds(pl.multiple_of(seg(pan, t, h, k, i), PR), PR)

    def step1(p):
        pan = PANELS[p]
        s = (z + 4) % N_Z
        for h in (0, 1):

            def one(k, i, b):
                st[ring_rows(pan, 0, h, k, i), :] = piece(pan, k, s, b).astype(BF)

            over(pan, h, s, one)
            ring(p, 1, far(h), h).start()

    def step(p, t, h):
        pan = PANELS[p]
        order = ("d", "u") if far(h) == "u" else ("u", "d")
        for way in order:
            buf = rsd if way == "d" else rsu
            dist = 5 - t
            s = (z + N_Z - dist) % N_Z if way == "d" else (z + dist) % N_Z
            fresh = t == 2 and way != far(h)
            if not fresh:
                ring(p, t - 1, way, h).wait_recv()

            def one(k, i, b):
                r = ring_rows(pan, t - 2, h, k, i)
                own = piece(pan, k, s, b)
                if not fresh:
                    own = own + buf[r, :].astype(F32)
                buf[r, :] = own.astype(BF)

            over(pan, h, s, one)
            ring(p, t, way, h).start()

    def slot(pan, q, k=0):
        return pan["ub"] * N_DP + q * (pan["J"] + 1) + k

    def slots(pan, q, count):
        return pl.ds(slot(pan, q), count)

    def ringed(b, owner):
        return (b // 2 + N_DP // 2 - owner // 2) % (N_DP // 2) < DIAG

    def by_count(pan, has, fn):
        @pl.when(has)
        def _():
            fn(pan["J"] + 1)

        if pan["J"] > 0:

            @pl.when(jnp.logical_not(has))
            def _():
                fn(pan["J"])

    def place(pan, q, count):
        return (
            pl.ds(pan["ub"], count),
            pl.ds(pl.multiple_of((q % 2) * PR, PR), PR),
            pl.ds(pl.multiple_of((q // 2) * PC, PC), PC),
        )

    def finish(p):
        pan = PANELS[p]
        for h in (0, 1):
            ring(p, 4, "d", h).wait_recv()
            ring(p, 4, "u", h).wait_recv()

            def one(k, i, b):
                r = ring_rows(pan, 3, h, k, i)
                v = piece(pan, k, z, b) + rsd[r, :].astype(F32) + rsu[r, :].astype(F32)
                ts[slot(pan, b, k)] = v.astype(BF)

            over(pan, h, z, one)

        def one_peer(r, c):
            b = (dp + r) % N_DP

            def send(count):
                remote(
                    ts.at[slots(pan, b, count)],
                    tx.at[slots(pan, dp, count)],
                    x_send.at[p],
                    x_recv.at[p],
                    (b, ex),
                ).start()

            by_count(pan, ringed(b, z), send)
            return c

        lax.fori_loop(1, N_DP, one_peer, 0)

        def keep(count):
            tx[slots(pan, dp, count)] = ts[slots(pan, dp, count)]

        by_count(pan, ringed(dp, z), keep)

    def turn(p):
        pan = PANELS[p]
        wait_equal(pan, x_recv.at[p])

        def move(count):
            def one_peer(r, c):
                q, dev = line_peer(r)
                remote(
                    tx.at[slots(pan, q, count)],
                    tr.at[place(pan, z, count)],
                    z_send.at[p],
                    z_recv.at[p],
                    dev,
                ).start()
                return c

            lax.fori_loop(1, N_Z, one_peer, 0)
            tr[place(pan, z, count)] = tx[slots(pan, z, count)]

        by_count(pan, ringed(dp, z), move)

    def wait_equal(pan, sem):
        by_count(pan, ringed(dp, z), lambda count: wait_slots((N_DP - 1) * count, sem))

    def wait_mixed(pan, sem):
        most = (N_DP - 1) * (pan["J"] + 1)

        @pl.when(ringed(dp, z))
        def _():
            wait_slots(most - (N_DP - 2 * DIAG), sem)

        @pl.when(jnp.logical_not(ringed(dp, z)))
        def _():
            wait_slots(most - (N_DP - 2 * DIAG) + 1, sem)

    def wait_slots(count, sem):
        v = ts.at[pl.ds(0, count)]
        pltpu.make_async_copy(v, v, sem).wait()

    def put(pan, row, col, v):
        out, count = (of, NF) if pan["kind"] == "f" else (og, NG)
        v = v.astype(BF)
        for b in range(N_DP):
            c = (b * count + col) * SUB
            out[0, pl.ds(row * SUB, SUB), pl.ds(c, SUB)] = v[:, b * SUB : (b + 1) * SUB]

    def tile_slot(pan, b):
        return pan["tb"] * N_DP + b * pan["J"]

    def wait_tiles(j, sem):
        v = tt.at[pl.ds(0, (N_DP - 1) * j)]
        pltpu.make_async_copy(v, v, sem).wait()

    def spread(p):
        pan = PANELS[p]
        j = pan["J"]
        wait_mixed(pan, z_recv.at[p])
        if j > 0:
            mine = pl.ds(pan["ub"], j)
            dst = pl.ds(tile_slot(pan, dp), j)

            def one(r, c):
                b = (dp + r) % N_DP
                lanes = pl.ds(pl.multiple_of((b // 2) * 128, 128), 128)
                remote(
                    tr.at[mine, :, lanes], tt.at[dst], m_send.at[p], m_recv.at[p], (b, ex)
                ).start()
                return c

            lax.fori_loop(1, N_DP, one, 0)
            own_lanes = pl.ds(pl.multiple_of((dp // 2) * 128, 128), 128)
            tt[dst] = tr[mine, :, own_lanes]
        for i in (0, 1):
            e_copy(p, i).start()
        for k in range(j):
            put(pan, j, k, tr[pan["ub"] + k])

    def e_copy(p, i):
        pan = PANELS[p]
        m = (dp // 2 + N_DP // 2 - 1) % (N_DP // 2)
        lanes = pl.ds(pl.multiple_of(m * 128, 128), 128)
        return remote(
            tr.at[pan["ub"] + pan["J"], :, lanes],
            td.at[p * 2 + dp % 2],
            e_send.at[p],
            e_recv.at[p],
            (m * 2 + i, ex),
        )

    def wait_diag(sem):
        v = td.at[pl.ds(0, 2)]
        pltpu.make_async_copy(v, v, sem).wait()

    def collect(p):
        pan = PANELS[p]
        j = pan["J"]
        off = (dp % 2) * SUB
        pick = lax.broadcasted_iota(jnp.int32, (SUB, 128), 1) == (
            lax.broadcasted_iota(jnp.int32, (SUB, 128), 0) + off
        )
        pick = jnp.where(pick, 1.0, 0.0).astype(BF)
        wait_diag(e_recv.at[p])
        tiles = jnp.concatenate([td[p * 2], td[p * 2 + 1]], axis=0)
        v = lax.dot_general(pick, tiles, (((1,), (1,)), ((), ())), preferred_element_type=F32)
        parts = []
        for m in range(N_DP // 2):
            have = tr[pan["ub"] + j, :, m * 128 : (m + 1) * 128].astype(F32)
            parts.append(jnp.where((dp // 2 + 1) % (N_DP // 2) == m, v, have))
        put(pan, j, j, jnp.concatenate(parts, axis=1))
        if j > 0:
            wait_tiles(j, m_recv.at[p])
        for k in range(j):
            parts = [tt[tile_slot(pan, b) + k] for b in range(N_DP)]
            tiles = jnp.concatenate(parts, axis=0)
            v = lax.dot_general(pick, tiles, (((1,), (1,)), ((), ())), preferred_element_type=F32)
            put(pan, k, j, v)

    def land(p):
        wait_rows(rb, (E - 1) * CAP, a_recv.at[p])

    build(0)
    pl.semaphore_wait(barrier, E - 1 + N_Z - 1)
    push(0)
    for p in range(1, AHEAD):
        build(p)
        push(p)
    lax.fori_loop(0, ROWS // chunk, select_pairs, 0)
    scale_grads()

    def front(p):
        land(p)
        if p + AHEAD < NP:
            build(p + AHEAD)
            push(p + AHEAD)
        compute(p)
        step1(p)

    for kind, p, h in make_order():
        if kind == "land":
            front(p)
        elif kind == "sum":
            finish(p)
        elif kind == "turn":
            turn(p)
        elif kind == "out":
            spread(p)
        elif kind == "tile":
            collect(p)
        else:
            step(p, kind, h)

    for p in range(NP):
        wait_rows(sb, (E - 1) * CAP, a_send.at[p])
        for h in (0, 1):
            ring(p, 1, far(h), h).wait_send()
            for t in (2, 3, 4):
                ring(p, t, "d", h).wait_send()
                ring(p, t, "u", h).wait_send()
        wait_mixed(PANELS[p], x_send.at[p])
        wait_equal(PANELS[p], z_send.at[p])
        j = PANELS[p]["J"]
        wait_diag(e_send.at[p])
        if j > 0:
            wait_tiles(j, m_send.at[p])


def finalize(f_in, g_in, f_out, g_out):
    f_out[...] = f_in[...].astype(F32) * SCALE
    g_out[...] = g_in[...].astype(F32) * SCALE


def per_device(features, expert_ids, gate_weights, out_grads):
    tokens, width = features.shape
    routes, hidden = out_grads.shape[1:]
    pairs = routes * tokens
    nf, ng = width // W, hidden // W
    vm = pl.BlockSpec(memory_space=pltpu.VMEM)
    hbm = pl.BlockSpec(memory_space=pl.ANY)
    dma = pltpu.SemaphoreType.DMA
    of, og = pl.pallas_call(
        kernel,
        out_shape=(
            jax.ShapeDtypeStruct((1, nf * SUB, width), BF),
            jax.ShapeDtypeStruct((1, ng * SUB, hidden), BF),
        ),
        in_specs=[vm, hbm, vm, vm],
        out_specs=(vm, vm),
        scratch_shapes=[
            pltpu.VMEM((tokens, routes, hidden), BF),
            pltpu.VMEM((pairs, hidden), BF),
            pltpu.VMEM((tokens, W), BF),
            pltpu.VMEM((pairs, W), BF),
            pltpu.VMEM((ROWS, pairs), BF),
            pltpu.VMEM((ROWS, tokens), BF),
            pltpu.VMEM((NP * ROWS, W), BF),
            pltpu.VMEM((NP * ROWS, W), BF),
            pltpu.VMEM((UNITS * W, W), F32),
            pltpu.VMEM((4 * PIECES * PR, PC), BF),
            pltpu.VMEM((4 * PIECES * PR, PC), BF),
            pltpu.VMEM((PIECES * PR, PC), BF),
            pltpu.VMEM((UNITS * N_DP, PR, PC), BF),
            pltpu.VMEM((UNITS * N_DP, PR, PC), BF),
            pltpu.VMEM((UNITS, SUB, W), BF),
            pltpu.VMEM((TUNITS * N_DP, SUB, 128), BF),
            pltpu.VMEM((NP * 2, SUB, 128), BF),
            dma((NP,)),
            dma((NP,)),
            dma((NP * 8,)),
            dma((NP * 8,)),
            dma((NP * 8,)),
            dma((NP * 8,)),
            dma,
            dma((NP,)),
            dma((NP,)),
            dma((NP,)),
            dma((NP,)),
            dma((NP,)),
            dma((NP,)),
            dma((NP,)),
            dma((NP,)),
        ],
        compiler_params=pltpu.CompilerParams(
            collective_id=0, has_side_effects=True, vmem_limit_bytes=60 * 1024 * 1024
        ),
        cost_estimate=pl.CostEstimate(
            flops=9_000_000_000, bytes_accessed=8_000_000, transcendentals=0
        ),
    )(features, out_grads, gate_weights.T, expert_ids.T)
    steps = 4

    def block(x):
        return pl.BlockSpec((1, x.shape[1] // steps, x.shape[2]), lambda i: (0, i, 0))

    return pl.pallas_call(
        finalize,
        grid=(steps,),
        out_shape=tuple(jax.ShapeDtypeStruct(x.shape, F32) for x in (of, og)),
        in_specs=[block(of), block(og)],
        out_specs=(block(of), block(og)),
    )(of, og)


def solution(mesh):
    in_specs = (
        P(("dp", "expert"), None),
        P(("dp", "expert"), None),
        P(("dp", "expert"), None),
        P(("dp", "expert"), None, None),
    )
    out_specs = (P("expert", "dp", None), P("expert", "dp", None))
    return jax.shard_map(
        per_device, mesh=mesh, in_specs=in_specs, out_specs=out_specs, check_vma=False
    )
```

```python
import jax
import jax.numpy as jnp
from jax import lax
from jax.experimental import pallas as pl
from jax.experimental.pallas import tpu as pltpu
from jax.sharding import PartitionSpec as P

MESH = pl.DeviceIdType.MESH
BF = jnp.bfloat16
F32 = jnp.float32

N_DP = 8
N_Z = 8
N_Y = 4
E = 32
CAP = 32
ROWS = E * CAP
W = 512
SUB = 64
SCALE = 1.0 / 1024.0


PR, PC = 32, 128
HALF = N_DP // 2
DIAG = 3


def half_pieces(j):
    return j * HALF + DIAG


def make_panels(nf, ng):
    panels = []
    ub = tb = rb = 0
    for kind, count in (("f", nf), ("g", ng)):
        for j in range(count):
            panels.append(dict(kind=kind, J=j, ub=ub, tb=tb, rb=rb, first=len(panels) - j))
            ub += j + 1
            tb += j
            rb += 2 * half_pieces(j)
    return panels, ub, tb, rb


NF, NG = 4, 3
PANELS, UNITS, TUNITS, PIECES = make_panels(NF, NG)
NP = len(PANELS)
AHEAD = 2


def make_order(first=8.0, every=15.0, hop=1.6, lag=2.5, move_lag=4.0, x_lag=15.0):
    ready = {("land", p, 0): first + every * (p + 1) for p in range(NP)}
    link = now = 0.0
    order = []
    halves = dict.fromkeys(range(NP), 0)
    while ready:
        now = max(now, min(ready.values()))
        op = min(ready, key=lambda o: (ready[o] - (4.0 if o[1] >= 5 else 0.0), o[1], str(o[0]), o[2]))
        del ready[op]
        order.append(op)
        kind, p, h = op
        size = PANELS[p]["J"] + 1
        ring_size = PANELS[p]["J"] + 0.75
        if kind == "land":
            now += 1.3 * size + 3.0
            for h in (0, 1):
                link = max(link, now) + 0.25 * hop * ring_size
                ready[(2, p, h)] = link + lag
        elif kind == "sum":
            now += 0.3 * size + 0.3
            ready[("turn", p, 0)] = now + 0.5 * size + x_lag
        elif kind == "turn":
            now += 0.3
            link = max(link, now) + hop * size
            ready[("out", p, 0)] = link + move_lag
        elif kind == "out":
            now += 0.3 * size + 0.3
            ready[("tile", p, 0)] = now + x_lag + size
        elif kind == "tile":
            now += 0.5 * size
        else:
            now += 0.2 * size + 0.15
            link = max(link, now) + 0.5 * hop * ring_size
            if kind < 4:
                ready[(kind + 1, p, h)] = link + lag
            else:
                halves[p] += 1
                if halves[p] == 2:
                    ready[("sum", p, 0)] = link + lag
    return order


def kernel(
    feats, raw, gates, ids, of, og,
    grads, scaled, panel_f, panel_g, sel, self_f, sb, rb, gram, rsd, rsu, st, ts, tx, tr, tt, td,
    a_send, a_recv, d_send, d_recv, u_send, u_recv,
    raw_sem, x_send, x_recv, z_send, z_recv, m_send, m_recv, e_send, e_recv,
):
    dp = lax.axis_index("dp")
    ex = lax.axis_index("expert")
    z = ex // N_Y
    y = ex % N_Y
    me = dp * N_Y + y

    def plane_peer(r):
        q = (me + r) % E
        return q, (q // N_Y, z * N_Y + q % N_Y)

    def line_peer(r):
        q = (z + r) % N_Z
        return q, (dp, q * N_Y + y)

    down = (dp, ((z + N_Z - 1) % N_Z) * N_Y + y)
    up = (dp, ((z + 1) % N_Z) * N_Y + y)

    raw_copy = pltpu.make_async_copy(raw, grads, raw_sem)
    raw_copy.start()
    barrier = pltpu.get_barrier_semaphore()

    def greet(r, c):
        pl.semaphore_signal(barrier, inc=1, device_id=plane_peer(r)[1], device_id_type=MESH)
        return c

    def greet_line(r, c):
        pl.semaphore_signal(barrier, inc=1, device_id=line_peer(r)[1], device_id_type=MESH)
        return c

    lax.fori_loop(1, E, greet, 0)
    lax.fori_loop(1, N_Z, greet_line, 0)

    tokens = feats.shape[0]
    routes = gates.shape[0]
    pairs = routes * tokens
    idv = jnp.concatenate([ids[k : k + 1, :] for k in range(routes)], axis=1)

    def iota(shape, dim):
        return lax.broadcasted_iota(jnp.int32, shape, dim)

    def ones_where(m):
        return jnp.where(m, 1.0, 0.0)

    hot = ones_where(iota((E, pairs), 0) == idv)
    tri = ones_where(iota((pairs, pairs), 0) < iota((pairs, pairs), 1)).astype(BF)
    earlier = jnp.dot(hot.astype(BF), tri, preferred_element_type=F32)
    pos = jnp.sum(earlier * hot, axis=0, keepdims=True)
    target = idv * CAP + pos.astype(jnp.int32)
    chunk = 128

    def select_tokens(i, c):
        r0 = pl.multiple_of(i * chunk, chunk)
        m = ones_where(iota((chunk, pairs), 0) + r0 == target)
        both = sum(m[:, k * tokens : (k + 1) * tokens] for k in range(routes))
        self_f[pl.ds(r0, chunk), :] = both.astype(BF)
        return c

    lax.fori_loop(0, ROWS // chunk, select_tokens, 0)

    def select_pairs(i, c):
        r0 = pl.multiple_of(i * chunk, chunk)
        sel[pl.ds(r0, chunk), :] = ones_where(iota((chunk, pairs), 0) + r0 == target).astype(BF)
        return c

    def scale_grads():
        raw_copy.wait()
        weights = [jnp.broadcast_to(gates[k : k + 1, :], (128, tokens)).T for k in range(routes)]
        for i in range(grads.shape[2] // 128):
            lanes = slice(i * 128, (i + 1) * 128)
            for k in range(routes):
                v = grads[:, k, lanes].astype(F32) * weights[k]
                scaled[k * tokens : (k + 1) * tokens, lanes] = v.astype(BF)

    def gather_columns(pan, ref, b):
        count = NG if pan["kind"] == "g" else NF
        at = [((b + i) * count + pan["J"]) * SUB for i in (0, 1)]
        return [ref[:, pl.ds(a, SUB)] for a in at]

    def arrange(p):
        pan = PANELS[p]
        src, dst = (feats, panel_f) if pan["kind"] == "f" else (scaled, panel_g)
        for m in range(N_DP // 2):
            lanes = slice(2 * SUB * m, 2 * SUB * (m + 1))
            dst[:, lanes] = jnp.concatenate(gather_columns(pan, src, 2 * m), axis=1)

    def build(p):
        pan = PANELS[p]
        arrange(p)
        src = panel_f if pan["kind"] == "f" else panel_g
        pick = self_f if pan["kind"] == "f" else sel

        def one(i, c):
            r0 = pl.multiple_of(i * 256, 256)
            v = jnp.dot(pick[pl.ds(r0, 256), :], src[...], preferred_element_type=F32)
            sb[pl.ds(pl.multiple_of(p * ROWS + r0, 256), 256), :] = v.astype(BF)
            return c

        lax.fori_loop(0, ROWS // 256, one, 0)
        own = pl.multiple_of(p * ROWS + me * CAP, CAP)
        rb[pl.ds(own, CAP), :] = sb[pl.ds(own, CAP), :]

    def push(p):
        def one(r, c):
            q, dev = plane_peer(r)
            pltpu.make_async_remote_copy(
                src_ref=sb.at[pl.ds(pl.multiple_of(p * ROWS + q * CAP, CAP), CAP), :],
                dst_ref=rb.at[pl.ds(pl.multiple_of(p * ROWS + me * CAP, CAP), CAP), :],
                send_sem=a_send.at[p],
                recv_sem=a_recv.at[p],
                device_id=dev,
                device_id_type=MESH,
            ).start()
            return c

        lax.fori_loop(1, E, one, 0)

    def wait_rows(ref, rows, sem):
        v = ref.at[pl.ds(0, rows), :]
        pltpu.make_async_copy(v, v, sem).wait()

    def compute(p):
        pan = PANELS[p]
        f0 = pan["first"]

        def one(i, c):
            k = i // 2
            h = i % 2
            a = rb[pl.ds(p * ROWS, ROWS), pl.ds(pl.multiple_of(h * 256, 256), 256)]
            b = rb[pl.ds(pl.multiple_of((f0 + k) * ROWS, ROWS), ROWS), :]
            v = lax.dot_general(a, b, (((0,), (0,)), ((), ())), preferred_element_type=F32)
            gram[pl.ds(pl.multiple_of((pan["ub"] + k) * W + h * 256, 256), 256), :] = v
            return c

        lax.fori_loop(0, 2 * (pan["J"] + 1), one, 0)

    def piece(pan, k, s, b):
        r = (pan["ub"] + k) * W + b * SUB + (s % 2) * PR
        lanes = pl.ds(pl.multiple_of((s // 2) * PC, PC), PC)
        return gram[pl.ds(pl.multiple_of(r, PR), PR), lanes]

    def seg(pan, t, h, k=0, i=0):
        return (t * PIECES + pan["rb"] + h * half_pieces(pan["J"]) + k * HALF + i) * PR

    def height(pan):
        return half_pieces(pan["J"]) * PR

    def remote(src, dst, ss, rs, dev):
        return pltpu.make_async_remote_copy(
            src_ref=src, dst_ref=dst, send_sem=ss, recv_sem=rs, device_id=dev, device_id_type=MESH
        )

    def ring(p, t, way, h):
        pan = PANELS[p]
        buf, ss, rs, dev = (
            (rsd, d_send, d_recv, down) if way == "d" else (rsu, u_send, u_recv, up)
        )
        n = height(pan)
        if t == 1:
            src = st.at[pl.ds(seg(pan, 0, h), n), :]
        else:
            src = buf.at[pl.ds(seg(pan, t - 2, h), n), :]
        dst = buf.at[pl.ds(seg(pan, t - 1, h), n), :]
        i = (p * 4 + t - 1) * 2 + h
        return remote(src, dst, ss.at[i], rs.at[i], dev)

    def over(pan, h, s, fn):
        def one(k, c):
            for i in range(HALF):
                fn(k, i, h * HALF + i)
            return c

        lax.fori_loop(0, pan["J"], one, 0)
        for i in range(DIAG):
            fn(pan["J"], i, (s // 2 * 2 + h * DIAG + i) % N_DP)

    def far(h):
        return "d" if h == 0 else "u"

    def ring_rows(pan, t, h, k, i):
        return pl.ds(pl.multiple_of(seg(pan, t, h, k, i), PR), PR)

    def step1(p):
        pan = PANELS[p]
        s = (z + 4) % N_Z
        for h in (0, 1):

            def one(k, i, b):
                st[ring_rows(pan, 0, h, k, i), :] = piece(pan, k, s, b).astype(BF)

            over(pan, h, s, one)
            ring(p, 1, far(h), h).start()

    def step(p, t, h):
        pan = PANELS[p]
        order = ("d", "u") if far(h) == "u" else ("u", "d")
        for way in order:
            buf = rsd if way == "d" else rsu
            dist = 5 - t
            s = (z + N_Z - dist) % N_Z if way == "d" else (z + dist) % N_Z
            fresh = t == 2 and way != far(h)
            if not fresh:
                ring(p, t - 1, way, h).wait_recv()

            def one(k, i, b):
                r = ring_rows(pan, t - 2, h, k, i)
                own = piece(pan, k, s, b)
                if not fresh:
                    own = own + buf[r, :].astype(F32)
                buf[r, :] = own.astype(BF)

            over(pan, h, s, one)
            ring(p, t, way, h).start()

    def slot(pan, q, k=0):
        return pan["ub"] * N_DP + q * (pan["J"] + 1) + k

    def slots(pan, q, count):
        return pl.ds(slot(pan, q), count)

    def ringed(b, owner):
        return (b // 2 + N_DP // 2 - owner // 2) % (N_DP // 2) < DIAG

    def by_count(pan, has, fn):
        @pl.when(has)
        def _():
            fn(pan["J"] + 1)

        if pan["J"] > 0:

            @pl.when(jnp.logical_not(has))
            def _():
                fn(pan["J"])

    def place(pan, q, count):
        return (
            pl.ds(pan["ub"], count),
            pl.ds(pl.multiple_of((q % 2) * PR, PR), PR),
            pl.ds(pl.multiple_of((q // 2) * PC, PC), PC),
        )

    def finish(p):
        pan = PANELS[p]
        for h in (0, 1):
            ring(p, 4, "d", h).wait_recv()
            ring(p, 4, "u", h).wait_recv()

            def one(k, i, b):
                r = ring_rows(pan, 3, h, k, i)
                v = piece(pan, k, z, b) + rsd[r, :].astype(F32) + rsu[r, :].astype(F32)
                ts[slot(pan, b, k)] = v.astype(BF)

            over(pan, h, z, one)

        def one_peer(r, c):
            b = (dp + r) % N_DP

            def send(count):
                remote(
                    ts.at[slots(pan, b, count)],
                    tx.at[slots(pan, dp, count)],
                    x_send.at[p],
                    x_recv.at[p],
                    (b, ex),
                ).start()

            by_count(pan, ringed(b, z), send)
            return c

        lax.fori_loop(1, N_DP, one_peer, 0)

        def keep(count):
            tx[slots(pan, dp, count)] = ts[slots(pan, dp, count)]

        by_count(pan, ringed(dp, z), keep)

    def turn(p):
        pan = PANELS[p]
        wait_equal(pan, x_recv.at[p])

        def move(count):
            def one_peer(r, c):
                q, dev = line_peer(r)
                remote(
                    tx.at[slots(pan, q, count)],
                    tr.at[place(pan, z, count)],
                    z_send.at[p],
                    z_recv.at[p],
                    dev,
                ).start()
                return c

            lax.fori_loop(1, N_Z, one_peer, 0)
            tr[place(pan, z, count)] = tx[slots(pan, z, count)]

        by_count(pan, ringed(dp, z), move)

    def wait_equal(pan, sem):
        by_count(pan, ringed(dp, z), lambda count: wait_slots((N_DP - 1) * count, sem))

    def wait_mixed(pan, sem):
        most = (N_DP - 1) * (pan["J"] + 1)

        @pl.when(ringed(dp, z))
        def _():
            wait_slots(most - (N_DP - 2 * DIAG), sem)

        @pl.when(jnp.logical_not(ringed(dp, z)))
        def _():
            wait_slots(most - (N_DP - 2 * DIAG) + 1, sem)

    def wait_slots(count, sem):
        v = ts.at[pl.ds(0, count)]
        pltpu.make_async_copy(v, v, sem).wait()

    def put(pan, row, col, v):
        out, count = (of, NF) if pan["kind"] == "f" else (og, NG)
        v = v.astype(BF)
        for b in range(N_DP):
            c = (b * count + col) * SUB
            out[0, pl.ds(row * SUB, SUB), pl.ds(c, SUB)] = v[:, b * SUB : (b + 1) * SUB]

    def tile_slot(pan, b):
        return pan["tb"] * N_DP + b * pan["J"]

    def wait_tiles(j, sem):
        v = tt.at[pl.ds(0, (N_DP - 1) * j)]
        pltpu.make_async_copy(v, v, sem).wait()

    def spread(p):
        pan = PANELS[p]
        j = pan["J"]
        wait_mixed(pan, z_recv.at[p])
        if j > 0:
            mine = pl.ds(pan["ub"], j)
            dst = pl.ds(tile_slot(pan, dp), j)

            def one(r, c):
                b = (dp + r) % N_DP
                lanes = pl.ds(pl.multiple_of((b // 2) * 128, 128), 128)
                remote(
                    tr.at[mine, :, lanes], tt.at[dst], m_send.at[p], m_recv.at[p], (b, ex)
                ).start()
                return c

            lax.fori_loop(1, N_DP, one, 0)
            own_lanes = pl.ds(pl.multiple_of((dp // 2) * 128, 128), 128)
            tt[dst] = tr[mine, :, own_lanes]
        for i in (0, 1):
            e_copy(p, i).start()
        for k in range(j):
            put(pan, j, k, tr[pan["ub"] + k])

    def e_copy(p, i):
        pan = PANELS[p]
        m = (dp // 2 + N_DP // 2 - 1) % (N_DP // 2)
        lanes = pl.ds(pl.multiple_of(m * 128, 128), 128)
        return remote(
            tr.at[pan["ub"] + pan["J"], :, lanes],
            td.at[p * 2 + dp % 2],
            e_send.at[p],
            e_recv.at[p],
            (m * 2 + i, ex),
        )

    def wait_diag(sem):
        v = td.at[pl.ds(0, 2)]
        pltpu.make_async_copy(v, v, sem).wait()

    def collect(p):
        pan = PANELS[p]
        j = pan["J"]
        off = (dp % 2) * SUB
        pick = lax.broadcasted_iota(jnp.int32, (SUB, 128), 1) == (
            lax.broadcasted_iota(jnp.int32, (SUB, 128), 0) + off
        )
        pick = jnp.where(pick, 1.0, 0.0).astype(BF)
        wait_diag(e_recv.at[p])
        tiles = jnp.concatenate([td[p * 2], td[p * 2 + 1]], axis=0)
        v = lax.dot_general(pick, tiles, (((1,), (1,)), ((), ())), preferred_element_type=F32)
        parts = []
        for m in range(N_DP // 2):
            have = tr[pan["ub"] + j, :, m * 128 : (m + 1) * 128].astype(F32)
            parts.append(jnp.where((dp // 2 + 1) % (N_DP // 2) == m, v, have))
        put(pan, j, j, jnp.concatenate(parts, axis=1))
        if j > 0:
            wait_tiles(j, m_recv.at[p])
        for k in range(j):
            parts = [tt[tile_slot(pan, b) + k] for b in range(N_DP)]
            tiles = jnp.concatenate(parts, axis=0)
            v = lax.dot_general(pick, tiles, (((1,), (1,)), ((), ())), preferred_element_type=F32)
            put(pan, k, j, v)

    def land(p):
        wait_rows(rb, (E - 1) * CAP, a_recv.at[p])

    build(0)
    pl.semaphore_wait(barrier, E - 1 + N_Z - 1)
    push(0)
    for p in range(1, AHEAD):
        build(p)
        push(p)
    lax.fori_loop(0, ROWS // chunk, select_pairs, 0)
    scale_grads()
    build(AHEAD)

    def front(p):
        land(p)
        if p + AHEAD < NP:
            push(p + AHEAD)
        compute(p)
        step1(p)
        if p + AHEAD + 1 < NP:
            build(p + AHEAD + 1)

    for kind, p, h in make_order():
        if kind == "land":
            front(p)
        elif kind == "sum":
            finish(p)
        elif kind == "turn":
            turn(p)
        elif kind == "out":
            spread(p)
        elif kind == "tile":
            collect(p)
        else:
            step(p, kind, h)

    for p in range(NP):
        wait_rows(sb, (E - 1) * CAP, a_send.at[p])
        for h in (0, 1):
            ring(p, 1, far(h), h).wait_send()
            for t in (2, 3, 4):
                ring(p, t, "d", h).wait_send()
                ring(p, t, "u", h).wait_send()
        wait_mixed(PANELS[p], x_send.at[p])
        wait_equal(PANELS[p], z_send.at[p])
        j = PANELS[p]["J"]
        wait_diag(e_send.at[p])
        if j > 0:
            wait_tiles(j, m_send.at[p])


def finalize(f_in, g_in, f_out, g_out):
    f_out[...] = f_in[...].astype(F32) * SCALE
    g_out[...] = g_in[...].astype(F32) * SCALE


def per_device(features, expert_ids, gate_weights, out_grads):
    tokens, width = features.shape
    routes, hidden = out_grads.shape[1:]
    pairs = routes * tokens
    nf, ng = width // W, hidden // W
    vm = pl.BlockSpec(memory_space=pltpu.VMEM)
    hbm = pl.BlockSpec(memory_space=pl.ANY)
    dma = pltpu.SemaphoreType.DMA
    of, og = pl.pallas_call(
        kernel,
        out_shape=(
            jax.ShapeDtypeStruct((1, nf * SUB, width), BF),
            jax.ShapeDtypeStruct((1, ng * SUB, hidden), BF),
        ),
        in_specs=[vm, hbm, vm, vm],
        out_specs=(vm, vm),
        scratch_shapes=[
            pltpu.VMEM((tokens, routes, hidden), BF),
            pltpu.VMEM((pairs, hidden), BF),
            pltpu.VMEM((tokens, W), BF),
            pltpu.VMEM((pairs, W), BF),
            pltpu.VMEM((ROWS, pairs), BF),
            pltpu.VMEM((ROWS, tokens), BF),
            pltpu.VMEM((NP * ROWS, W), BF),
            pltpu.VMEM((NP * ROWS, W), BF),
            pltpu.VMEM((UNITS * W, W), F32),
            pltpu.VMEM((4 * PIECES * PR, PC), BF),
            pltpu.VMEM((4 * PIECES * PR, PC), BF),
            pltpu.VMEM((PIECES * PR, PC), BF),
            pltpu.VMEM((UNITS * N_DP, PR, PC), BF),
            pltpu.VMEM((UNITS * N_DP, PR, PC), BF),
            pltpu.VMEM((UNITS, SUB, W), BF),
            pltpu.VMEM((TUNITS * N_DP, SUB, 128), BF),
            pltpu.VMEM((NP * 2, SUB, 128), BF),
            dma((NP,)),
            dma((NP,)),
            dma((NP * 8,)),
            dma((NP * 8,)),
            dma((NP * 8,)),
            dma((NP * 8,)),
            dma,
            dma((NP,)),
            dma((NP,)),
            dma((NP,)),
            dma((NP,)),
            dma((NP,)),
            dma((NP,)),
            dma((NP,)),
            dma((NP,)),
        ],
        compiler_params=pltpu.CompilerParams(
            collective_id=0, has_side_effects=True, vmem_limit_bytes=60 * 1024 * 1024
        ),
        cost_estimate=pl.CostEstimate(
            flops=9_000_000_000, bytes_accessed=8_000_000, transcendentals=0
        ),
    )(features, out_grads, gate_weights.T, expert_ids.T)
    steps = 4

    def block(x):
        return pl.BlockSpec((1, x.shape[1] // steps, x.shape[2]), lambda i: (0, i, 0))

    return pl.pallas_call(
        finalize,
        grid=(steps,),
        out_shape=tuple(jax.ShapeDtypeStruct(x.shape, F32) for x in (of, og)),
        in_specs=[block(of), block(og)],
        out_specs=(block(of), block(og)),
    )(of, og)


def solution(mesh):
    in_specs = (
        P(("dp", "expert"), None),
        P(("dp", "expert"), None),
        P(("dp", "expert"), None),
        P(("dp", "expert"), None, None),
    )
    out_specs = (P("expert", "dp", None), P("expert", "dp", None))
    return jax.shard_map(
        per_device, mesh=mesh, in_specs=in_specs, out_specs=out_specs, check_vma=False
    )
```
